512 devices in a mesh: run: 16 (over y, x_lo), fsdp: 32 (over x_hi, z, core).
Axes of the slice: x: 4 (x_hi: 2, x_lo: 2; x = x_hi * 2 + x_lo), y: 8, z: 8, core: 2. Of those that a mesh axis runs over, the one named last changes fastest.
Arguments:
- table: bfloat16 [256, 4608], P('fsdp', 'run'), may hold values from -6 to 6
- token_ids: int32 [4, 128], P(None, 'fsdp'), may hold values from 0 to 255
- cotangent: bfloat16 [4, 128, 4608], P(None, 'fsdp', 'run'), may hold values from -6 to 6
- gate_weight: bfloat16 [4, 4608, 18432], P(None, 'run', 'fsdp'), may hold values from -6 to 6
- up_weight: bfloat16 [4, 4608, 18432], P(None, 'run', 'fsdp'), may hold values from -6 to 6
- down_weight: bfloat16 [4, 4608, 18432], P(None, 'run', 'fsdp'), may hold values from -6 to 6
Outputs:
- merged_gate: bfloat16 [4608, 18432], P('run', 'fsdp')
- merged_up: bfloat16 [4608, 18432], P('run', 'fsdp')
- merged_down: bfloat16 [4608, 18432], P('run', 'fsdp')
The draws below stay inside these ranges and needn't reach their ends.
All inputs are finite; a program needn't handle non-finite values.
Results may differ from the reference program's by a relative error of at most 0.039.
Values may be sent and summed in bfloat16 or wider, within the bound.
A program may use at most 64 MiB of HBM per device.

```python
import jax
import jax.numpy as jnp
from jax import lax

D = 4608
FF = 18432
RUNS = 4
ENTRIES = 256
TOKENS_RUN = 128
N_RUN = 16


def with_ends(entries, stream_key, least, top_value):
    place = [jax.random.randint(jax.random.fold_in(stream_key, axis), (), 0, length) for axis, length in enumerate(entries.shape)]
    longest = entries.shape.index(max(entries.shape))
    next_to = place[:longest] + [(place[longest] + 1) % entries.shape[longest]] + place[longest + 1:]
    return entries.at[tuple(place)].set(least).at[tuple(next_to)].set(top_value)


def level_of(key, shape, split, least, largest):
    def one(dim, parts):
        draws = jax.random.uniform(jax.random.fold_in(jax.random.fold_in(key, 6), dim), (parts,), jnp.float32, least / len(split), largest / len(split))
        return jnp.repeat(jnp.exp(draws), shape[dim] // parts).reshape((-1,) + (1,) * (len(shape) - dim - 1))

    gain = one(*split[0])
    for cut in split[1:]:
        gain = gain * one(*cut)
    return gain


def noise(rng, shape, deviation, bound, cuts=(), dtype=jnp.bfloat16):
    values = jax.random.normal(rng, shape, jnp.float32) * deviation
    if len(cuts) > 0:
        values = level_of(rng, shape, cuts, -0.22, 0.18) * values
    return jnp.clip(values, min=-bound, max=bound).astype(dtype)


def setup_inputs(seed: int = 0) -> dict:
    key_of = jax.random.split(jax.random.key(seed), 7)
    table = noise(key_of[0], (ENTRIES, D), 1.0, 6.0, ((0, 32), (1, 16)))
    token_ids = with_ends(jax.random.randint(key_of[1], (RUNS, TOKENS_RUN), 0, ENTRIES), jax.random.fold_in(key_of[1], 1), 0, ENTRIES - 1).astype(jnp.int32)
    cotangent = noise(key_of[2], (RUNS, TOKENS_RUN, D), 1.0, 6.0, ((1, 32), (2, 16)))
    gate_weight = noise(key_of[3], (RUNS, D, FF), 1.0, 6.0, ((1, 16), (2, 32)))
    up_weight = noise(key_of[4], (RUNS, D, FF), 1.0, 6.0, ((1, 16), (2, 32)))
    down_weight = noise(key_of[5], (RUNS, D, FF), 1.0, 6.0, ((1, 16), (2, 32)))
    return dict(table=table, token_ids=token_ids, cotangent=cotangent, gate_weight=gate_weight, up_weight=up_weight, down_weight=down_weight)


PRIOR = 0.01


def gelu_tanh(value):
    return jax.nn.gelu(value, approximate=True)


def block_sum(left, right, factor):
    width = D // N_RUN
    count = left.shape[0]
    left_blocks = left.reshape(count, N_RUN, width).transpose(1, 0, 2)
    right_blocks = right.reshape(N_RUN, width, right.shape[1])

    def add_term(total, pair):
        part_left, part_right = pair
        term = (jnp.dot(part_left, part_right, preferred_element_type=jnp.float32) * factor).astype(jnp.bfloat16)
        term = lax.optimization_barrier(term)
        return total + term.astype(jnp.float32), None

    start = jnp.zeros((count, right.shape[1]), jnp.float32)
    total, _ = lax.scan(add_term, start, (left_blocks, right_blocks))
    return total


def run_fisher(table, ids, cot, w_gate, w_up, w_down):
    rows = jnp.take(table, ids, axis=0)
    gate = block_sum(rows, w_gate, D ** -0.5)
    up = block_sum(rows, w_up, D ** -0.5)
    back = block_sum(cot, w_down, FF ** -0.5)
    act, slope = jax.jvp(gelu_tanh, (gate,), (jnp.ones_like(gate),))
    hidden = (act * up).astype(jnp.bfloat16)
    d_gate = (back * up * slope).astype(jnp.bfloat16)
    d_up = (back * act).astype(jnp.bfloat16)
    grad_gate = jnp.dot(rows.T, d_gate, preferred_element_type=jnp.float32) * (D ** -0.5)
    grad_up = jnp.dot(rows.T, d_up, preferred_element_type=jnp.float32) * (D ** -0.5)
    grad_down = jnp.dot(cot.T, hidden, preferred_element_type=jnp.float32) * (FF ** -0.5)
    return ((grad_gate * grad_gate).astype(jnp.bfloat16),
            (grad_up * grad_up).astype(jnp.bfloat16),
            (grad_down * grad_down).astype(jnp.bfloat16))


def reference(table, token_ids, cotangent, gate_weight, up_weight, down_weight):
    def step(carry, inputs):
        ids, cot, w_gate, w_up, w_down = inputs
        fishers = run_fisher(table, ids, cot, w_gate, w_up, w_down)
        weights = (w_gate, w_up, w_down)
        numers, denoms = carry
        new_numers = []
        new_denoms = []
        for index in range(3):
            factor = fishers[index].astype(jnp.float32) + PRIOR
            new_numers.append(numers[index] + factor * weights[index].astype(jnp.float32))
            new_denoms.append(denoms[index] + factor)
        return (tuple(new_numers), tuple(new_denoms)), None

    zeros = jnp.zeros((D, FF), jnp.float32)
    start = ((zeros, zeros, zeros), (zeros, zeros, zeros))
    (numers, denoms), _ = lax.scan(step, start, (token_ids, cotangent, gate_weight, up_weight, down_weight))
    return ((numers[0] / denoms[0]).astype(jnp.bfloat16),
            (numers[1] / denoms[1]).astype(jnp.bfloat16),
            (numers[2] / denoms[2]).astype(jnp.bfloat16))
```

```python
import jax
import jax.numpy as jnp
from jax import lax
from jax.experimental import pallas as pl
from jax.experimental.pallas import tpu as pltpu
from jax.sharding import PartitionSpec as P

D = 4608
FF = 18432
PRIOR = 0.01
DB = 288
FB = 576
RUNS = 4
TOK = 128
NY = 8
MESH = pl.DeviceIdType.MESH
BF = jnp.bfloat16
F32 = jnp.float32
WIDTH = (768, 1024)
ORDER = (4, 3, 5, 2, 6, 1, 7)


def dot(a, b):
    return jnp.dot(a, b, preferred_element_type=F32)


def iota(shape, dim):
    return lax.broadcasted_iota(jnp.int32, shape, dim)


def place(rows, shift):
    return (iota((rows, 128), 1) == iota((rows, 128), 0) + shift).astype(BF)


def kernel(
    ids_ref, table_ref, cot_ref, wg_hbm, wu_hbm, wd_hbm,
    og_ref, ou_ref, od_ref,
    wg, wu, wd, wt, m1, m2, rows_s, cot_s, rows_t, cot_t, tbl,
    sx0, sx1, rx0, rx1, own0, own1, sy0, sy1, ry0, ry1, h0, h1,
    num_g, num_u, num_d, num_t, den_g, den_u, den_d, den_t,
    w_sem, g_send, g_recv, f_send, f_recv,
    x_send, x_recv, y_send, y_recv, ay_send, ay_recv, ax_send, ax_recv,
):
    sx, rx, own, sy, ry, hb = (sx0, sx1), (rx0, rx1), (own0, own1), (sy0, sy1), (ry0, ry1), (h0, h1)
    run, fs = lax.axis_index("run"), lax.axis_index("fsdp")
    y, xl = run // 2, run % 2
    chip, core = fs // 2, fs % 2
    xh, z = chip // 8, chip % 8

    def y_peer(k):
        return (lax.rem(y + k, NY) * 2 + xl, fs)

    x_peer = (y * 2 + 1 - xl, fs)
    sibling = (run, chip * 2 + 1 - core)
    gather_peers = []
    for dz in (4, 3, 5, 2, 6, 1, 7, 0):
        for dx in (1, 0):
            if dz or dx:
                other = lax.rem(xh + dx, 2) * 8 + lax.rem(z + dz, 8)
                gather_peers.append((run, other * 2 + core))

    barrier = pltpu.get_barrier_semaphore()
    everyone = gather_peers + [sibling, x_peer] + [y_peer(k) for k in ORDER]
    for peer in everyone:
        pl.semaphore_signal(barrier, inc=1, device_id=peer, device_id_type=MESH)

    weight_copies = []
    for i, (src, dst) in enumerate(((wg_hbm, wg), (wu_hbm, wu), (wd_hbm, wd))):
        copy = pltpu.make_async_copy(src, dst, w_sem.at[i])
        copy.start()
        weight_copies.append(copy)

    table = table_ref[...].astype(F32)
    cot = jnp.concatenate([cot_ref[r].astype(F32) for r in range(RUNS)], axis=0)
    ids = jnp.zeros((16, 128), F32)
    row, lane = iota((16, 128), 0), iota((16, 128), 1)
    for r in range(RUNS):
        for t in range(4):
            ids = jnp.where((row == 4 * r + t) & (lane == 64), ids_ref[r, t].astype(F32), ids)
    tail = dot(cot[:, 256:288].astype(BF), place(32, 32))
    table_tail = dot(table[:, 256:288].astype(BF), place(32, 0))
    tail = tail + ids + jnp.concatenate([table_tail, jnp.zeros((8, 128), F32)], axis=0)
    folded = jnp.concatenate([table[:, 0:128], table[:, 128:256]], axis=0)
    m1[core, chip] = jnp.concatenate([folded, tail], axis=1).astype(BF)
    m2[core, chip] = cot[:, 0:256].astype(BF)

    pl.semaphore_wait(barrier, len(everyone))

    sends = []

    def send(src, dst, s_sem, r_sem, peer):
        copy = pltpu.make_async_remote_copy(
            src_ref=src, dst_ref=dst, send_sem=s_sem, recv_sem=r_sem, device_id=peer, device_id_type=MESH
        )
        copy.start()
        sends.append(copy)
        return copy

    gathers = []
    for j, buf in enumerate((m1, m2)):
        gathers.append([
            send(buf.at[core, chip], buf.at[core, chip], g_send.at[j, i], g_recv.at[j, i], peer)
            for i, peer in enumerate(gather_peers)
        ])

    for copy in weight_copies:
        copy.wait()
    for r in range(RUNS):
        wt[r] = jnp.concatenate([wg[r, :, 512:576], wu[r, :, 512:576]], axis=1)

    def finish_gather(j, buf):
        for copy in gathers[j]:
            copy.wait_recv()
        fwd = send(buf.at[core], buf.at[core], f_send.at[j], f_recv.at[j], sibling)
        fwd.wait_recv()

    def picker(r):
        i, g = iota((TOK, 512), 0), iota((TOK, 512), 1)
        return (g == 16 * (i // 4) + 4 * r + i % 4).astype(BF)

    finish_gather(0, m1)
    m1f = m1[...].astype(F32).reshape(32, 16, 256)
    tbl[:, 0:128] = m1f[:, 0:8, 0:128].reshape(256, 128).astype(BF)
    tbl[:, 128:256] = m1f[:, 8:16, 0:128].reshape(256, 128).astype(BF)
    tbl[:, 256:384] = m1f[:, 0:8, 128:256].reshape(256, 128).astype(BF)

    def pick_rows(r):
        z_tail = dot(picker(r), m1[...].reshape(512, 256)[:, 128:256])
        j = iota((TOK, 256), 1)
        entry = ((j % 128) // 8) * 16 + (j // 128) * 8 + j % 8
        hot = (z_tail[:, 64:65].astype(jnp.int32) == entry).astype(BF)
        rows = dot(hot, tbl[...])
        rows_s[r] = rows.astype(BF)
        rows_t[r] = rows.T.astype(BF)
        cot_tail = pltpu.roll(z_tail, 96, 1)
        cot_s[r, :, 256:384] = cot_tail.astype(BF)
        cot_t[r, 256:384, :] = cot_tail.T.astype(BF)

    def pick_cot(r):
        main = dot(picker(r), m2[...].reshape(512, 256))
        cot_s[r, :, 0:256] = main.astype(BF)
        cot_t[r, 0:256, :] = main.T.astype(BF)

    def forward_gu(r, h, out):
        rows = rows_s[r, :, 0:DB]
        cols = slice(256 * h, 256 * h + 256)
        out[:, 0:256] = (dot(rows, wg[r, :, cols]) * D ** -0.5).astype(out.dtype)
        out[:, 256:512] = (dot(rows, wu[r, :, cols]) * D ** -0.5).astype(out.dtype)
        if h == 1:
            out[:, 768:896] = (dot(rows, wt[r]) * D ** -0.5).astype(out.dtype)

    def forward_b(r, h, out):
        cots = cot_s[r, :, 0:DB]
        out[:, 512:768] = (dot(cots, wd[r, :, 256 * h:256 * h + 256]) * FF ** -0.5).astype(out.dtype)
        if h == 1:
            last = dot(cots, wd[r, :, 512:576]) * FF ** -0.5
            out[:, 896:1024] = jnp.concatenate([last, jnp.zeros_like(last)], axis=1).astype(out.dtype)

    def start_x(p, h):
        return send(sx[h].at[p], rx[h].at[p], x_send.at[p, h], x_recv.at[p, h], x_peer)

    exchanges = {}
    theirs, mine = (1 - xl, 3 - xl), (xl, 2 + xl)
    pick_rows(theirs[0])
    forward_gu(theirs[0], 0, sx[0].at[0])
    finish_gather(1, m2)
    pick_cot(theirs[0])
    forward_b(theirs[0], 0, sx[0].at[0])
    exchanges[0, 0] = start_x(0, 0)
    forward_gu(theirs[0], 1, sx[1].at[0])
    forward_b(theirs[0], 1, sx[1].at[0])
    exchanges[0, 1] = start_x(0, 1)
    pick_rows(mine[0])
    pick_cot(mine[0])
    for h in range(2):
        forward_gu(mine[0], h, own[h].at[0])
        forward_b(mine[0], h, own[h].at[0])
    pick_rows(theirs[1])
    pick_cot(theirs[1])
    for h in range(2):
        forward_gu(theirs[1], h, sx[h].at[1])
        forward_b(theirs[1], h, sx[h].at[1])
        exchanges[1, h] = start_x(1, h)
    pick_rows(mine[1])
    pick_cot(mine[1])
    for h in range(2):
        forward_gu(mine[1], h, own[h].at[1])
        forward_b(mine[1], h, own[h].at[1])

    my_rows = pl.ds(pl.multiple_of(16 * y, 16), 16)
    scatters, spreads, relays = {}, {}, {}

    def reduce_x(p, h):
        exchanges[p, h].wait_recv()
        sy[h][p] = (own[h][p] + rx[h][p].astype(F32)).astype(BF)
        scatters[p, h] = []
        for k in ORDER:
            to = lax.rem(y + k, NY)
            src = sy[h].at[p, pl.ds(pl.multiple_of(16 * to, 16), 16)]
            scatters[p, h].append(
                send(src, ry[h].at[p, k - 1], y_send.at[p, h, k - 1], y_recv.at[p, h, k - 1], y_peer(k))
            )

    def act_grads(gate, up, back):
        c = 0.7978845608028654
        inner = c * (gate + 0.044715 * gate * gate * gate)
        th = jnp.tanh(inner)
        half = 0.5 * (1.0 + th)
        act = gate * half
        slope = half + 0.5 * gate * (1.0 - th * th) * c * (1.0 + 3 * 0.044715 * gate * gate)
        return act * up, back * up * slope, back * act

    def reduce_y(p, h):
        for copy in scatters[p, h]:
            copy.wait_recv()
        total = sy[h][p, my_rows, :].astype(F32)
        for k in range(NY - 1):
            total = total + ry[h][p, k].astype(F32)
        hidden, d_gate, d_up = act_grads(total[:, 0:256], total[:, 256:512], total[:, 512:768])
        parts = [d_gate, d_up, hidden]
        if h == 1:
            both, back = total[:, 768:896], total[:, 896:1024]
            hidden, d_gate, d_up = act_grads(both, pltpu.roll(both, 64, 1), back)
            low = iota((16, 128), 1) < 64
            parts.append(jnp.where(low, d_gate, pltpu.roll(d_up, 64, 1)))
            parts.append(jnp.where(low, hidden, 0.0))
        r = mine[p]
        hb[h][r, my_rows, :] = jnp.concatenate(parts, axis=1).astype(BF)
        block = hb[h].at[r, my_rows]
        spreads[p, h] = [
            send(block, block, ay_send.at[p, h, k - 1], ay_recv.at[p, h, k - 1], y_peer(k)) for k in ORDER
        ]
        relays[p, h] = [send(block, block, ax_send.at[p, h, 0], ax_recv.at[p, h, 0], x_peer)]

    def relay(p, h):
        for k, copy in reversed(list(zip(ORDER, spreads[p, h]))):
            copy.wait_recv()
            source = lax.rem(y + NY - k, NY)
            block = hb[h].at[mine[p], pl.ds(pl.multiple_of(16 * source, 16), 16)]
            relays[p, h].append(send(block, block, ax_send.at[p, h, k], ax_recv.at[p, h, k], x_peer))

    def merge(p, h):
        for copy in relays[p, h]:
            copy.wait_recv()
        cols = slice(256 * h, 256 * h + 256)
        whole = slice(0, 128)
        jobs = [
            (rows_t, slice(0, 256), wg, cols, num_g, den_g, 1.0 / D, og_ref),
            (rows_t, slice(256, 512), wu, cols, num_u, den_u, 1.0 / D, ou_ref),
            (cot_t, slice(512, 768), wd, cols, num_d, den_d, 1.0 / FF, od_ref),
        ]
        if h == 1:
            jobs.append((rows_t, slice(768, 896), wt, whole, num_t, den_t, 1.0 / D, None))
            jobs.append((cot_t, slice(896, 960), wd, slice(512, 576), num_d, den_d, 1.0 / FF, od_ref))
        for left, lanes, weight, cols, num, den, scale, out in jobs:
            n, d = None, None
            for r in (2 * p, 2 * p + 1):
                grad = dot(left[r, 0:DB, :], hb[h][r, :, lanes])
                factor = grad * grad * scale + PRIOR
                term = factor * weight[r, :, cols].astype(F32)
                n, d = (term, factor) if n is None else (n + term, d + factor)
            if p == 0:
                num[:, cols] = n
                den[:, cols] = d
                continue
            merged = ((num[:, cols] + n) / (den[:, cols] + d)).astype(BF)
            if out is None:
                og_ref[:, 512:576] = merged[:, 0:64]
                ou_ref[:, 512:576] = merged[:, 64:128]
            else:
                out[:, cols] = merged

    units = [(0, 0), (0, 1), (1, 0), (1, 1)]
    for slot in range(len(units) + 3):
        for lag, stage in enumerate((reduce_x, reduce_y, relay, merge)):
            if 0 <= slot - lag < len(units):
                stage(*units[slot - lag])

    for copy in sends:
        copy.wait_send()


def on_device(table, token_ids, cotangent, gate_weight, up_weight, down_weight):
    vm = pl.BlockSpec(memory_space=pltpu.VMEM)
    hbm = pl.BlockSpec(memory_space=pl.ANY)
    weight = pltpu.VMEM((RUNS, DB, FB), BF)
    sem = pltpu.SemaphoreType.DMA

    def both(lead, dtype):
        return [pltpu.VMEM(lead + (w,), dtype) for w in WIDTH]

    return pl.pallas_call(
        kernel,
        out_shape=[jax.ShapeDtypeStruct((DB, FB), BF)] * 3,
        in_specs=[pl.BlockSpec(memory_space=pltpu.SMEM), vm, vm, hbm, hbm, hbm],
        out_specs=[vm] * 3,
        scratch_shapes=[
            weight, weight, weight, pltpu.VMEM((RUNS, DB, 128), BF),
            pltpu.VMEM((2, 16, 16, 256), BF), pltpu.VMEM((2, 16, 16, 256), BF),
            pltpu.VMEM((RUNS, TOK, 384), BF), pltpu.VMEM((RUNS, TOK, 384), BF),
            pltpu.VMEM((RUNS, 384, TOK), BF), pltpu.VMEM((RUNS, 384, TOK), BF),
            pltpu.VMEM((256, 384), BF),
            *both((2, TOK), BF), *both((2, TOK), BF), *both((2, TOK), F32), *both((2, TOK), BF),
            *both((2, NY - 1, 16), BF), *both((RUNS, TOK), BF),
            *([pltpu.VMEM((DB, FB), F32)] * 3), pltpu.VMEM((DB, 128), F32),
            *([pltpu.VMEM((DB, FB), F32)] * 3), pltpu.VMEM((DB, 128), F32),
            sem((3,)), sem((2, 15)), sem((2, 15)), sem((2,)), sem((2,)),
            sem((2, 2)), sem((2, 2)), sem((2, 2, 7)), sem((2, 2, 7)),
            sem((2, 2, 7)), sem((2, 2, 7)), sem((2, 2, 8)), sem((2, 2, 8)),
        ],
        compiler_params=pltpu.CompilerParams(
            collective_id=0, has_side_effects=True, vmem_limit_bytes=48 * 1024 * 1024
        ),
        cost_estimate=pl.CostEstimate(flops=1100000000, bytes_accessed=5200000, transcendentals=300000),
    )(token_ids, table, cotangent, gate_weight, up_weight, down_weight)


def solution(mesh):
    return jax.shard_map(
        on_device,
        mesh=mesh,
        in_specs=(
            P("fsdp", "run"),
            P(None, "fsdp"),
            P(None, "fsdp", "run"),
            P(None, "run", "fsdp"),
            P(None, "run", "fsdp"),
            P(None, "run", "fsdp"),
        ),
        out_specs=(P("run", "fsdp"), P("run", "fsdp"), P("run", "fsdp")),
        check_vma=False,
    )
```

```python
import jax
import jax.numpy as jnp
from jax import lax
from jax.experimental import pallas as pl
from jax.experimental.pallas import tpu as pltpu
from jax.sharding import PartitionSpec as P

D = 4608
FF = 18432
PRIOR = 0.01
DB = 288
FB = 576
RUNS = 4
TOK = 128
NY = 8
MESH = pl.DeviceIdType.MESH
BF = jnp.bfloat16
F32 = jnp.float32
WIDTH = (768, 1024)
GU = (512, 640)
LAGS = (0.0, 4.0, 8.0, 12.0, 16.0, 20.0)


def dot(a, b):
    return jnp.dot(a, b, preferred_element_type=F32)


def iota(shape, dim):
    return lax.broadcasted_iota(jnp.int32, shape, dim)


def place(rows, shift):
    return (iota((rows, 128), 1) == iota((rows, 128), 0) + shift).astype(BF)


def kernel(
    ids_ref, table_ref, cot_ref, wg_hbm, wu_hbm, wd_hbm,
    og_ref, ou_ref, od_ref,
    wg, wu, wd, wt, m1, m2, rows_s, cot_s, rows_t, cot_t, tbl,
    sx0, sx1, rx0, rx1, own0, own1, sy0, sy1, ry0, ry1, cy0, cy1, h0, h1,
    num_g, num_u, num_d, num_t, den_g, den_u, den_d, den_t,
    w_sem, g_send, g_recv, f_send, f_recv,
    x_send, x_recv, y_send, y_recv, ay_send, ay_recv, ax_send, ax_recv,
):
    sx, rx, own, sy = (sx0, sx1), (rx0, rx1), (own0, own1), (sy0, sy1)
    ry, cy, hb = (ry0, ry1), (cy0, cy1), (h0, h1)
    run, fs = lax.axis_index("run"), lax.axis_index("fsdp")
    y, xl = run // 2, run % 2
    chip, core = fs // 2, fs % 2
    xh, z = chip // 8, chip % 8

    def y_peer(k):
        return (lax.rem(y + k, NY) * 2 + xl, fs)

    x_peer = (y * 2 + 1 - xl, fs)
    sibling = (run, chip * 2 + 1 - core)
    gather_peers = []
    for dz in (4, 3, 5, 2, 6, 1, 7, 0):
        for dx in (1, 0):
            if dz or dx:
                other = lax.rem(xh + dx, 2) * 8 + lax.rem(z + dz, 8)
                gather_peers.append((run, other * 2 + core))

    barrier = pltpu.get_barrier_semaphore()
    everyone = gather_peers + [sibling, x_peer] + [y_peer(k) for k in (2, 6, 1, 7)]
    for peer in everyone:
        pl.semaphore_signal(barrier, inc=1, device_id=peer, device_id_type=MESH)

    weight_copies = []
    for i, (src, dst) in enumerate(((wg_hbm, wg), (wu_hbm, wu), (wd_hbm, wd))):
        copy = pltpu.make_async_copy(src, dst, w_sem.at[i])
        copy.start()
        weight_copies.append(copy)

    table = table_ref[...].astype(F32)
    cot = jnp.concatenate([cot_ref[r].astype(F32) for r in range(RUNS)], axis=0)
    ids = jnp.zeros((16, 128), F32)
    row, lane = iota((16, 128), 0), iota((16, 128), 1)
    for r in range(RUNS):
        for t in range(4):
            ids = jnp.where((row == 4 * r + t) & (lane == 64), ids_ref[r, t].astype(F32), ids)
    tail = dot(cot[:, 256:288].astype(BF), place(32, 32))
    table_tail = dot(table[:, 256:288].astype(BF), place(32, 0))
    tail = tail + ids + jnp.concatenate([table_tail, jnp.zeros((8, 128), F32)], axis=0)
    folded = jnp.concatenate([table[:, 0:128], table[:, 128:256]], axis=0)
    m1[core, chip] = jnp.concatenate([folded, tail], axis=1).astype(BF)
    m2[core, chip] = cot[:, 0:256].astype(BF)

    pl.semaphore_wait(barrier, len(everyone))

    sends = []

    def send(src, dst, s_sem, r_sem, peer):
        copy = pltpu.make_async_remote_copy(
            src_ref=src, dst_ref=dst, send_sem=s_sem, recv_sem=r_sem, device_id=peer, device_id_type=MESH
        )
        copy.start()
        sends.append(copy)
        return copy

    gathers = []
    for j, buf in enumerate((m1, m2)):
        gathers.append([
            send(buf.at[core, chip], buf.at[core, chip], g_send.at[j, i], g_recv.at[j, i], peer)
            for i, peer in enumerate(gather_peers)
        ])

    for copy in weight_copies:
        copy.wait()
    for r in range(RUNS):
        wt[r] = jnp.concatenate([wg[r, :, 512:576], wu[r, :, 512:576]], axis=1)

    def finish_gather(j, buf):
        for copy in gathers[j]:
            copy.wait_recv()
        fwd = send(buf.at[core], buf.at[core], f_send.at[j], f_recv.at[j], sibling)
        fwd.wait_recv()

    def picker(r):
        i, g = iota((TOK, 512), 0), iota((TOK, 512), 1)
        return (g == 16 * (i // 4) + 4 * r + i % 4).astype(BF)

    finish_gather(0, m1)
    m1f = m1[...].astype(F32).reshape(32, 16, 256)
    tbl[:, 0:128] = m1f[:, 0:8, 0:128].reshape(256, 128).astype(BF)
    tbl[:, 128:256] = m1f[:, 8:16, 0:128].reshape(256, 128).astype(BF)
    tbl[:, 256:384] = m1f[:, 0:8, 128:256].reshape(256, 128).astype(BF)

    def pick_rows(r):
        z_tail = dot(picker(r), m1[...].reshape(512, 256)[:, 128:256])
        j = iota((TOK, 256), 1)
        entry = ((j % 128) // 8) * 16 + (j // 128) * 8 + j % 8
        hot = (z_tail[:, 64:65].astype(jnp.int32) == entry).astype(BF)
        rows = dot(hot, tbl[...])
        rows_s[r] = rows.astype(BF)
        rows_t[r] = rows.T.astype(BF)
        cot_tail = pltpu.roll(z_tail, 96, 1)
        cot_s[r, :, 256:384] = cot_tail.astype(BF)
        cot_t[r, 256:384, :] = cot_tail.T.astype(BF)

    def pick_cot(r):
        main = dot(picker(r), m2[...].reshape(512, 256))
        cot_s[r, :, 0:256] = main.astype(BF)
        cot_t[r, 0:256, :] = main.T.astype(BF)

    def forward_gu(r, h, out):
        rows = rows_s[r, :, 0:DB]
        cols = slice(256 * h, 256 * h + 256)
        out[:, 0:256] = (dot(rows, wg[r, :, cols]) * D ** -0.5).astype(out.dtype)
        out[:, 256:512] = (dot(rows, wu[r, :, cols]) * D ** -0.5).astype(out.dtype)
        if h == 1:
            out[:, 512:640] = (dot(rows, wt[r]) * D ** -0.5).astype(out.dtype)

    def forward_b(r, h, out):
        cots = cot_s[r, :, 0:DB]
        out[:, GU[h]:GU[h] + 256] = (dot(cots, wd[r, :, 256 * h:256 * h + 256]) * FF ** -0.5).astype(out.dtype)
        if h == 1:
            last = dot(cots, wd[r, :, 512:576]) * FF ** -0.5
            out[:, 896:1024] = jnp.concatenate([last, jnp.zeros_like(last)], axis=1).astype(out.dtype)

    exchanges = {}
    theirs, mine = (1 - xl, 3 - xl), (xl, 2 + xl)

    def start_x(p, h, part):
        lanes = (pl.ds(0, GU[h]), pl.ds(GU[h], WIDTH[h] - GU[h]))[part]
        exchanges[p, h, part] = send(
            sx[h].at[p, :, lanes], rx[h].at[p, :, lanes], x_send.at[p, h, part], x_recv.at[p, h, part], x_peer
        )

    pick_rows(theirs[0])
    forward_gu(theirs[0], 0, sx[0].at[0])
    start_x(0, 0, 0)
    forward_gu(theirs[0], 1, sx[1].at[0])
    finish_gather(1, m2)
    pick_cot(theirs[0])
    forward_b(theirs[0], 0, sx[0].at[0])
    start_x(0, 0, 1)
    start_x(0, 1, 0)
    forward_b(theirs[0], 1, sx[1].at[0])
    start_x(0, 1, 1)
    pick_rows(mine[0])
    pick_cot(mine[0])
    for h in range(2):
        forward_gu(mine[0], h, own[h].at[0])
        forward_b(mine[0], h, own[h].at[0])
    pick_rows(theirs[1])
    pick_cot(theirs[1])
    for h in range(2):
        forward_gu(theirs[1], h, sx[h].at[1])
        start_x(1, h, 0)
        forward_b(theirs[1], h, sx[h].at[1])
        start_x(1, h, 1)
    pick_rows(mine[1])
    pick_cot(mine[1])
    for h in range(2):
        forward_gu(mine[1], h, own[h].at[1])
        forward_b(mine[1], h, own[h].at[1])

    def at(k):
        return pl.ds(pl.multiple_of(16 * lax.rem(y + NY + k, NY), 16), 16)

    scatters, spreads, relays = {}, {}, {}

    def sign(p, h):
        return 1 if (p + h) % 2 == 0 else -1

    def scatter(p, h, slot, src, to):
        scatters[p, h, slot] = send(
            src, ry[h].at[p, slot], y_send.at[p, h, slot], y_recv.at[p, h, slot], y_peer(to % NY)
        )

    def reduce_x(p, h):
        exchanges[p, h, 0].wait_recv()
        exchanges[p, h, 1].wait_recv()
        sy[h][p] = (own[h][p] + rx[h][p].astype(F32)).astype(BF)
        g = sign(p, h)
        for slot, owner, to in ((0, -4, -2), (1, -3, -1), (2, 3, 1), (3, -1, -1), (4, 1, 1)):
            scatter(p, h, slot, sy[h].at[p, at(g * owner)], g * to)

    def combine_y(p, h):
        g = sign(p, h)
        for i, (slots, owner) in enumerate((((0, 1), -2), ((2,), 2))):
            total = sy[h][p, at(g * owner), :].astype(F32)
            for slot in slots:
                scatters[p, h, slot].wait_recv()
                total = total + ry[h][p, slot].astype(F32)
            cy[h][p, i] = total.astype(BF)
            scatter(p, h, 5 + i, cy[h].at[p, i], g * owner)

    def act_grads(gate, up, back):
        c = 0.7978845608028654
        inner = c * (gate + 0.044715 * gate * gate * gate)
        th = jnp.tanh(inner)
        half = 0.5 * (1.0 + th)
        act = gate * half
        slope = half + 0.5 * gate * (1.0 - th * th) * c * (1.0 + 3 * 0.044715 * gate * gate)
        return act * up, back * up * slope, back * act

    def relay(p, h, slot, owner):
        block = hb[h].at[mine[p], at(owner)]
        relays[p, h].append(send(block, block, ax_send.at[p, h, slot], ax_recv.at[p, h, slot], x_peer))

    def spread(p, h, slot, owner, to):
        block = hb[h].at[mine[p], at(owner)]
        spreads[p, h, slot] = send(
            block, block, ay_send.at[p, h, slot], ay_recv.at[p, h, slot], y_peer(to % NY)
        )

    def finish_y(p, h):
        total = sy[h][p, at(0), :].astype(F32)
        for slot in (3, 4, 5, 6):
            scatters[p, h, slot].wait_recv()
            total = total + ry[h][p, slot].astype(F32)
        b = GU[h]
        hidden, d_gate, d_up = act_grads(total[:, 0:256], total[:, 256:512], total[:, b:b + 256])
        parts = [d_gate, d_up, hidden]
        if h == 1:
            both, back = total[:, 512:640], total[:, 896:1024]
            hidden, d_gate, d_up = act_grads(both, pltpu.roll(both, 64, 1), back)
            low = iota((16, 128), 1) < 64
            parts.insert(2, jnp.where(low, d_gate, pltpu.roll(d_up, 64, 1)))
            parts.append(jnp.where(low, hidden, 0.0))
        hb[h][mine[p], at(0), :] = jnp.concatenate(parts, axis=1).astype(BF)
        g = sign(p, h)
        for slot, to in ((0, 2), (1, -2), (2, 1), (3, -1)):
            spread(p, h, slot, 0, g * to)
        relays[p, h] = []
        relay(p, h, 7, 0)

    def pass_on(p, h):
        g = sign(p, h)
        spreads[p, h, 0].wait_recv()
        spread(p, h, 5, -2 * g, 2 * g)
        spread(p, h, 4, -2 * g, g)
        spreads[p, h, 1].wait_recv()
        spread(p, h, 6, 2 * g, -g)
        relay(p, h, 0, -2 * g)
        relay(p, h, 1, 2 * g)
        for slot, owner in ((2, -1), (3, 1)):
            spreads[p, h, slot].wait_recv()
            relay(p, h, slot, g * owner)

    def pass_last(p, h):
        g = sign(p, h)
        for slot, owner in ((4, -3), (6, 3), (5, -4)):
            spreads[p, h, slot].wait_recv()
            relay(p, h, slot, g * owner)

    def merge(p, h):
        for copy in relays[p, h]:
            copy.wait_recv()
        cols = slice(256 * h, 256 * h + 256)
        whole = slice(0, 128)
        jobs = [
            (rows_t, slice(0, 256), wg, cols, num_g, den_g, 1.0 / D, og_ref),
            (rows_t, slice(256, 512), wu, cols, num_u, den_u, 1.0 / D, ou_ref),
            (cot_t, slice(GU[h], GU[h] + 256), wd, cols, num_d, den_d, 1.0 / FF, od_ref),
        ]
        if h == 1:
            jobs.append((rows_t, slice(512, 640), wt, whole, num_t, den_t, 1.0 / D, None))
            jobs.append((cot_t, slice(896, 960), wd, slice(512, 576), num_d, den_d, 1.0 / FF, od_ref))
        for left, lanes, weight, cols, num, den, scale, out in jobs:
            n, d = None, None
            for r in (2 * p, 2 * p + 1):
                grad = dot(left[r, 0:DB, :], hb[h][r, :, lanes])
                factor = grad * grad * scale + PRIOR
                term = factor * weight[r, :, cols].astype(F32)
                n, d = (term, factor) if n is None else (n + term, d + factor)
            if p == 0:
                num[:, cols] = n
                den[:, cols] = d
                continue
            merged = ((num[:, cols] + n) / (den[:, cols] + d)).astype(BF)
            if out is None:
                og_ref[:, 512:576] = merged[:, 0:64]
                ou_ref[:, 512:576] = merged[:, 64:128]
            else:
                out[:, cols] = merged

    units = [(0, 0), (0, 1), (1, 0), (1, 1)]
    stages = (reduce_x, combine_y, finish_y, pass_on, pass_last, merge)
    arrival = (4.5, 10.0, 14.0, 19.5)
    events = [
        (arrival[i] + lag, i, j)
        for i in range(len(units))
        for j, lag in enumerate(LAGS)
    ]
    for _, i, j in sorted(events):
        stages[j](*units[i])

    for copy in sends:
        copy.wait_send()


def deliver(a, b, c, oa, ob, oc, sems):
    copies = [pltpu.make_async_copy(s, d, sems.at[i]) for i, (s, d) in enumerate(((a, oa), (b, ob), (c, oc)))]
    for copy in copies:
        copy.start()
    for copy in copies:
        copy.wait()


def on_device(table, token_ids, cotangent, gate_weight, up_weight, down_weight):
    vm = pl.BlockSpec(memory_space=pltpu.VMEM)
    hbm = pl.BlockSpec(memory_space=pl.ANY)
    weight = pltpu.VMEM((RUNS, DB, FB), BF)
    sem = pltpu.SemaphoreType.DMA

    def both(lead, dtype):
        return [pltpu.VMEM(lead + (w,), dtype) for w in WIDTH]

    merged = pl.pallas_call(
        kernel,
        out_shape=[jax.ShapeDtypeStruct((DB, FB), BF)] * 3,
        in_specs=[pl.BlockSpec(memory_space=pltpu.SMEM), vm, vm, hbm, hbm, hbm],
        out_specs=[vm] * 3,
        scratch_shapes=[
            weight, weight, weight, pltpu.VMEM((RUNS, DB, 128), BF),
            pltpu.VMEM((2, 16, 16, 256), BF), pltpu.VMEM((2, 16, 16, 256), BF),
            pltpu.VMEM((RUNS, TOK, 384), BF), pltpu.VMEM((RUNS, TOK, 384), BF),
            pltpu.VMEM((RUNS, 384, TOK), BF), pltpu.VMEM((RUNS, 384, TOK), BF),
            pltpu.VMEM((256, 384), BF),
            *both((2, TOK), BF), *both((2, TOK), BF), *both((2, TOK), F32), *both((2, TOK), BF),
            *both((2, NY - 1, 16), BF), *both((2, 2, 16), BF), *both((RUNS, TOK), BF),
            *([pltpu.VMEM((DB, FB), F32)] * 3), pltpu.VMEM((DB, 128), F32),
            *([pltpu.VMEM((DB, FB), F32)] * 3), pltpu.VMEM((DB, 128), F32),
            sem((3,)), sem((2, 15)), sem((2, 15)), sem((2,)), sem((2,)),
            sem((2, 2, 2)), sem((2, 2, 2)), sem((2, 2, 7)), sem((2, 2, 7)),
            sem((2, 2, 7)), sem((2, 2, 7)), sem((2, 2, 8)), sem((2, 2, 8)),
        ],
        compiler_params=pltpu.CompilerParams(
            collective_id=0, has_side_effects=True, vmem_limit_bytes=60 * 1024 * 1024
        ),
        cost_estimate=pl.CostEstimate(flops=1100000000, bytes_accessed=5200000, transcendentals=300000),
    )(token_ids, table, cotangent, gate_weight, up_weight, down_weight)
    return pl.pallas_call(
        deliver,
        out_shape=[jax.ShapeDtypeStruct((DB, FB), BF)] * 3,
        in_specs=[vm] * 3,
        out_specs=[hbm] * 3,
        scratch_shapes=[pltpu.SemaphoreType.DMA((3,))],
    )(*merged)


def solution(mesh):
    return jax.shard_map(
        on_device,
        mesh=mesh,
        in_specs=(
            P("fsdp", "run"),
            P(None, "fsdp"),
            P(None, "fsdp", "run"),
            P(None, "run", "fsdp"),
            P(None, "run", "fsdp"),
            P(None, "run", "fsdp"),
        ),
        out_specs=(P("run", "fsdp"), P("run", "fsdp"), P("run", "fsdp")),
        check_vma=False,
    )
```

```python
import jax
import jax.numpy as jnp
from jax import lax
from jax.experimental import pallas as pl
from jax.experimental.pallas import tpu as pltpu
from jax.sharding import PartitionSpec as P

D = 4608
FF = 18432
PRIOR = 0.01
DB = 288
FB = 576
RUNS = 4
TOK = 128
NY = 8
MESH = pl.DeviceIdType.MESH
BF = jnp.bfloat16
F32 = jnp.float32
BLOCKS = ((0, 256, 0), (256, 128, 0), (384, 128, 1))
UNITS = (
    (1, 2, True, False),
    (0, 0, False, False),
    (0, 2, True, False),
    (1, 0, False, False),
    (1, 1, False, False),
    (0, 1, False, True),
)
SIGNS = (-1, 1, 1, -1, -1, 1)
EARLY = (1,)
SCHEDULE = (
    (0, 1), (2, 1), (1, 0), (3, 0), (4, 0), (0, 2), (2, 2), (5, 0), (1, 1), (0, 3),
    (2, 3), (3, 1), (1, 2), (1, 3), (0, 5), (4, 1), (2, 5), (5, 1), (3, 2), (3, 3),
    (1, 5), (0, 6), (4, 2), (4, 3), (5, 2), (5, 3), (2, 6), (3, 5), (1, 6), (4, 5),
    (5, 4), (3, 6), (2, 7), (4, 6), (5, 5), (1, 7), (0, 7), (3, 7), (4, 7), (5, 6),
    (5, 7),
)


def gu_lanes(block):
    return 2 * block[1] + 128 * block[2]


def all_lanes(block):
    return 3 * block[1] + 256 * block[2]


def dot(a, b):
    return jnp.dot(a, b, preferred_element_type=F32)


def iota(shape, dim):
    return lax.broadcasted_iota(jnp.int32, shape, dim)


def place(rows, shift):
    return (iota((rows, 128), 1) == iota((rows, 128), 0) + shift).astype(BF)


def act_grads(gate, up, back):
    c = 0.7978845608028654
    inner = c * (gate + 0.044715 * gate * gate * gate)
    th = jnp.tanh(inner)
    half = 0.5 * (1.0 + th)
    act = gate * half
    slope = half + 0.5 * gate * (1.0 - th * th) * c * (1.0 + 3 * 0.044715 * gate * gate)
    return act * up, back * up * slope, back * act


def kernel(
    ids_ref, table_ref, cot_ref, wg_hbm, wu_hbm, wd_hbm,
    og_ref, ou_ref, od_ref,
    wg, wu, wd, wt, m1, m2, rows_s, cot_s, rows_t, cot_t, tbl,
    num_g, num_u, num_d, num_t, den_g, den_u, den_d, den_t,
    w_sem, g_send, g_recv, f_send, f_recv, x_send, x_recv, y_send, y_recv, c_send, c_recv,
    ay_send, ay_recv, ax_send, ax_recv, *bufs,
):
    n = len(UNITS)
    sx, rx, own, sy, ry, cy, ty, tb, rt, hb = (bufs[n * i:n * i + n] for i in range(10))
    run, fs = lax.axis_index("run"), lax.axis_index("fsdp")
    y, xl = run // 2, run % 2
    chip, core = fs // 2, fs % 2
    xh, z = chip // 8, chip % 8

    def y_peer(k):
        return (lax.rem(y + NY + k, NY) * 2 + xl, fs)

    x_peer = (y * 2 + 1 - xl, fs)
    sibling = (run, chip * 2 + 1 - core)
    gather_peers, gather_chips = [], []
    for dz in (4, 3, 5, 2, 6, 1, 7, 0):
        for dx in (1, 0):
            if dz or dx:
                to = lax.rem(xh + dx, 2) * 8 + lax.rem(z + dz, 8)
                gather_peers.append((run, to * 2 + core))
                gather_chips.append(lax.rem(xh + dx, 2) * 8 + lax.rem(z + 8 - dz, 8))

    barrier = pltpu.get_barrier_semaphore()
    everyone = gather_peers + [sibling, x_peer] + [y_peer(k) for k in (-2, 2, -1, 1)]
    for peer in everyone:
        pl.semaphore_signal(barrier, inc=1, device_id=peer, device_id_type=MESH)

    weight_copies = []
    for i, (src, dst) in enumerate(((wg_hbm, wg), (wu_hbm, wu), (wd_hbm, wd))):
        copy = pltpu.make_async_copy(src, dst, w_sem.at[i])
        copy.start()
        weight_copies.append(copy)

    table = table_ref[...].astype(F32)
    cot = jnp.concatenate([cot_ref[r].astype(F32) for r in range(RUNS)], axis=0)
    ids = jnp.zeros((16, 128), F32)
    row, lane = iota((16, 128), 0), iota((16, 128), 1)
    for r in range(RUNS):
        for t in range(4):
            ids = jnp.where((row == 4 * r + t) & (lane == 64), ids_ref[r, t].astype(F32), ids)
    tail = dot(cot[:, 256:288].astype(BF), place(32, 32))
    table_tail = dot(table[:, 256:288].astype(BF), place(32, 0))
    tail = tail + ids + jnp.concatenate([table_tail, jnp.zeros((8, 128), F32)], axis=0)
    folded = jnp.concatenate([table[:, 0:128], table[:, 128:256]], axis=0)
    m1[core, chip] = jnp.concatenate([folded, tail], axis=1).astype(BF)
    m2[core, chip] = cot[:, 0:256].astype(BF)

    pl.semaphore_wait(barrier, len(everyone))

    sends = []

    def send(src, dst, s_sem, r_sem, peer):
        copy = pltpu.make_async_remote_copy(
            src_ref=src, dst_ref=dst, send_sem=s_sem, recv_sem=r_sem, device_id=peer, device_id_type=MESH
        )
        copy.start()
        sends.append(copy)
        return copy

    def hand_over(j, buf, i, place):
        return send(buf.at[core, place], buf.at[core, place], f_send.at[j, i], f_recv.at[j, i], sibling)

    gathers = []
    for j, buf in enumerate((m1, m2)):
        gathers.append([
            send(buf.at[core, chip], buf.at[core, chip], g_send.at[j, i], g_recv.at[j, i], peer)
            for i, peer in enumerate(gather_peers)
        ])

    for copy in weight_copies:
        copy.wait()
    for r in range(RUNS):
        wt[r] = jnp.concatenate([wg[r, :, 512:576], wu[r, :, 512:576]], axis=1)

    def finish_gather(j, buf):
        handed = [hand_over(j, buf, 15, chip)]
        for i in reversed(range(15)):
            gathers[j][i].wait_recv()
            handed.append(hand_over(j, buf, i, gather_chips[i]))
        for copy in handed:
            copy.wait_recv()

    def picker(r):
        i, g = iota((TOK, 512), 0), iota((TOK, 512), 1)
        return (g == 16 * (i // 4) + 4 * r + i % 4).astype(BF)

    finish_gather(0, m1)
    m1f = m1[...].astype(F32).reshape(32, 16, 256)
    tbl[:, 0:128] = m1f[:, 0:8, 0:128].reshape(256, 128).astype(BF)
    tbl[:, 128:256] = m1f[:, 8:16, 0:128].reshape(256, 128).astype(BF)
    tbl[:, 256:384] = m1f[:, 0:8, 128:256].reshape(256, 128).astype(BF)

    def pick_rows(r):
        z_tail = dot(picker(r), m1[...].reshape(512, 256)[:, 128:256])
        j = iota((TOK, 256), 1)
        entry = ((j % 128) // 8) * 16 + (j // 128) * 8 + j % 8
        hot = (z_tail[:, 64:65].astype(jnp.int32) == entry).astype(BF)
        rows = dot(hot, tbl[...])
        rows_s[r] = rows.astype(BF)
        rows_t[r] = rows.T.astype(BF)
        cot_tail = pltpu.roll(z_tail, 96, 1)
        cot_s[r, :, 256:384] = cot_tail.astype(BF)
        cot_t[r, 256:384, :] = cot_tail.T.astype(BF)

    def pick_cot(r):
        main = dot(picker(r), m2[...].reshape(512, 256))
        cot_s[r, :, 0:256] = main.astype(BF)
        cot_t[r, 0:256, :] = main.T.astype(BF)

    def forward_gu(r, u, out):
        first, w, last = BLOCKS[UNITS[u][1]]
        rows = rows_s[r, :, 0:DB]
        out[:, 0:w] = (dot(rows, wg[r, :, first:first + w]) * D ** -0.5).astype(out.dtype)
        out[:, w:2 * w] = (dot(rows, wu[r, :, first:first + w]) * D ** -0.5).astype(out.dtype)
        if last:
            out[:, 2 * w:2 * w + 128] = (dot(rows, wt[r]) * D ** -0.5).astype(out.dtype)

    def forward_b(r, u, out):
        block = BLOCKS[UNITS[u][1]]
        first, w, last = block
        b = gu_lanes(block)
        cots = cot_s[r, :, 0:DB]
        out[:, b:b + w] = (dot(cots, wd[r, :, first:first + w]) * FF ** -0.5).astype(out.dtype)
        if last:
            left = dot(cots, wd[r, :, 512:576]) * FF ** -0.5
            out[:, b + w:b + w + 128] = jnp.concatenate([left, jnp.zeros_like(left)], axis=1).astype(out.dtype)

    exchanges, scatters, crossings, spreads, relays = {}, {}, {}, {}, {}

    def their_run(u):
        return 2 * UNITS[u][0] + 1 - xl

    def my_run(u):
        return 2 * UNITS[u][0] + xl

    def at(k):
        return pl.ds(pl.multiple_of(16 * lax.rem(y + NY + k, NY), 16), 16)

    def start_x(u, part):
        block = BLOCKS[UNITS[u][1]]
        b = gu_lanes(block)
        lanes = (pl.ds(0, b), pl.ds(b, all_lanes(block) - b))[part]
        exchanges[u, part] = send(
            sx[u].at[:, lanes], rx[u].at[:, lanes], x_send.at[u, part], x_recv.at[u, part], x_peer
        )

    def sign(u):
        return SIGNS[u]

    def scatter(u, slot, src, to):
        scatters[u, slot] = send(src, ry[u].at[slot], y_send.at[u, slot], y_recv.at[u, slot], y_peer(to))

    def scatter_first(u):
        g = sign(u)
        for slot, owner, to in ((0, -4, -2), (1, -3, -1), (2, 3, 1), (3, -1, -1), (4, 1, 1)):
            scatter(u, slot, sy[u].at[:, at(g * owner)], g * to)

    def reduce_x(u):
        if UNITS[u][2]:
            return
        exchanges[u, 0].wait_recv()
        exchanges[u, 1].wait_recv()
        sy[u][0] = (own[u][...] + rx[u][...].astype(F32)).astype(BF)
        scatter_first(u)

    def combine_y(u):
        g = sign(u)
        for i, (slots, owner) in enumerate((((0, 1), -2), ((2,), 2))):
            total = sy[u][:, at(g * owner), :].astype(F32)
            for slot in slots:
                scatters[u, slot].wait_recv()
                total = total + ry[u][slot].astype(F32)
            cy[u][i] = total.astype(BF)
            scatter(u, 5 + i, cy[u].at[i], g * owner)

    def finish_y(u):
        total = sy[u][:, at(0), :].astype(F32)
        for slot in (3, 4, 5, 6):
            scatters[u, slot].wait_recv()
            total = total + ry[u][slot].astype(F32)
        ty[u][...] = total
        if UNITS[u][2]:
            tb[u][...] = total.astype(BF)
            crossings[u] = send(tb[u].at[1 - xl], rt[u], c_send.at[u], c_recv.at[u], x_peer)

    def relay(u, slot, owner):
        block = hb[u].at[xl, at(owner)]
        relays[u].append(send(block, block, ax_send.at[u, slot], ax_recv.at[u, slot], x_peer))

    def spread(u, slot, owner, to):
        block = hb[u].at[:, at(owner)] if UNITS[u][3] else hb[u].at[xl, at(owner)]
        spreads[u, slot] = send(block, block, ay_send.at[u, slot], ay_recv.at[u, slot], y_peer(to))

    def activate(u):
        if UNITS[u][2]:
            crossings[u].wait_recv()
            total = ty[u][xl] + rt[u][...].astype(F32)
        else:
            total = ty[u][0]
        block = BLOCKS[UNITS[u][1]]
        w, b = block[1], gu_lanes(block)
        hidden, d_gate, d_up = act_grads(total[:, 0:w], total[:, w:2 * w], total[:, b:b + w])
        parts = [d_gate, d_up, hidden]
        if block[2]:
            both, back = total[:, 2 * w:2 * w + 128], total[:, b + w:b + w + 128]
            hidden, d_gate, d_up = act_grads(both, pltpu.roll(both, 64, 1), back)
            low = iota((16, 128), 1) < 64
            parts.insert(2, jnp.where(low, d_gate, pltpu.roll(d_up, 64, 1)))
            parts.append(jnp.where(low, hidden, 0.0))
        hb[u][xl, at(0), :] = jnp.concatenate(parts, axis=1).astype(BF)
        relays[u] = []
        if UNITS[u][3]:
            relay(u, 7, 0)
        else:
            spread_first(u)
            relay(u, 7, 0)

    def spread_first(u):
        g = sign(u)
        for slot, to in ((0, 2), (1, -2), (2, 1), (3, -1)):
            spread(u, slot, 0, g * to)

    def cross_back(u):
        if UNITS[u][3]:
            relays[u][0].wait_recv()
            spread_first(u)

    def pass_on(u):
        g = sign(u)
        spreads[u, 0].wait_recv()
        spread(u, 5, -2 * g, 2 * g)
        spread(u, 4, -2 * g, g)
        spreads[u, 1].wait_recv()
        spread(u, 6, 2 * g, -g)
        last = UNITS[u][3]
        if not last:
            relay(u, 0, -2 * g)
            relay(u, 1, 2 * g)
        for slot, owner in ((2, -1), (3, 1)):
            spreads[u, slot].wait_recv()
            if not last:
                relay(u, slot, g * owner)

    def pass_last(u):
        g = sign(u)
        for slot, owner in ((4, -3), (6, 3), (5, -4)):
            spreads[u, slot].wait_recv()
            if not UNITS[u][3]:
                relay(u, slot, g * owner)

    merged_pairs = {}

    def merge(u):
        if not UNITS[u][3]:
            for copy in relays[u]:
                copy.wait_recv()
        p, which = UNITS[u][:2]
        block = BLOCKS[which]
        first, w, last = block
        b = gu_lanes(block)
        cols = slice(first, first + w)
        jobs = [
            (rows_t, slice(0, w), wg, cols, num_g, den_g, 1.0 / D, og_ref),
            (rows_t, slice(w, 2 * w), wu, cols, num_u, den_u, 1.0 / D, ou_ref),
            (cot_t, slice(b, b + w), wd, cols, num_d, den_d, 1.0 / FF, od_ref),
        ]
        if last:
            jobs.append((rows_t, slice(2 * w, 2 * w + 128), wt, slice(0, 128), num_t, den_t, 1.0 / D, None))
            jobs.append((cot_t, slice(b + w, b + w + 64), wd, slice(512, 576), num_d, den_d, 1.0 / FF, od_ref))
        for left, lanes, weight, cols, num, den, scale, out in jobs:
            n, d = None, None
            for i in range(2):
                grad = dot(left[2 * p + i, 0:DB, :], hb[u][i, :, lanes])
                factor = grad * grad * scale + PRIOR
                term = factor * weight[2 * p + i, :, cols].astype(F32)
                n, d = (term, factor) if n is None else (n + term, d + factor)
            if which not in merged_pairs:
                num[:, cols] = n
                den[:, cols] = d
                continue
            merged = ((num[:, cols] + n) / (den[:, cols] + d)).astype(BF)
            if out is None:
                og_ref[:, 512:576] = merged[:, 0:64]
                ou_ref[:, 512:576] = merged[:, 64:128]
            else:
                out[:, cols] = merged
        merged_pairs[which] = True

    have_rows, have_cot, late = set(), set(), []

    def rows_for(key, r):
        if key not in have_rows:
            have_rows.add(key)
            pick_rows(r)

    def cot_for(key, r):
        if key not in have_cot:
            have_cot.add(key)
            pick_cot(r)

    def key_of(u, other):
        return (UNITS[u][0], other)

    def gu_send(u):
        if UNITS[u][2]:
            for i in range(2):
                rows_for(key_of(u, i), 2 * UNITS[u][0] + (xl if i else 1 - xl))
            for i, r in enumerate((their_run(u), my_run(u))):
                forward_gu(r, u, sy[u].at[(1 - xl) if i == 0 else xl])
        else:
            rows_for(key_of(u, 0), their_run(u))
            forward_gu(their_run(u), u, sx[u])
            start_x(u, 0)

    def b_send(u):
        if UNITS[u][2]:
            for i in range(2):
                cot_for(key_of(u, i), 2 * UNITS[u][0] + (xl if i else 1 - xl))
            for i, r in enumerate((their_run(u), my_run(u))):
                forward_b(r, u, sy[u].at[(1 - xl) if i == 0 else xl])
            scatter_first(u)
        else:
            cot_for(key_of(u, 0), their_run(u))
            forward_b(their_run(u), u, sx[u])
            start_x(u, 1)

    def keep(u):
        if not UNITS[u][2]:
            rows_for(key_of(u, 1), my_run(u))
            cot_for(key_of(u, 1), my_run(u))
            forward_gu(my_run(u), u, own[u])
            forward_b(my_run(u), u, own[u])

    for u in EARLY:
        gu_send(u)
    finish_gather(1, m2)
    for u in range(n):
        if u not in EARLY:
            gu_send(u)
        b_send(u)
    for u in range(n):
        keep(u)

    stages = (reduce_x, combine_y, finish_y, activate, cross_back, pass_on, pass_last, merge)
    for u, j in SCHEDULE:
        stages[j](u)

    for copy in sends:
        copy.wait_send()


def deliver(a, b, c, oa, ob, oc, sems):
    copies = [pltpu.make_async_copy(s, d, sems.at[i]) for i, (s, d) in enumerate(((a, oa), (b, ob), (c, oc)))]
    for copy in copies:
        copy.start()
    for copy in copies:
        copy.wait()


def on_device(table, token_ids, cotangent, gate_weight, up_weight, down_weight):
    vm = pl.BlockSpec(memory_space=pltpu.VMEM)
    hbm = pl.BlockSpec(memory_space=pl.ANY)
    weight = pltpu.VMEM((RUNS, DB, FB), BF)
    sem = pltpu.SemaphoreType.DMA
    n = len(UNITS)
    runs = [2 if unit[2] else 1 for unit in UNITS]

    def each(shape_of, dtype):
        return [
            pltpu.VMEM(shape_of(runs[u]) + (all_lanes(BLOCKS[UNITS[u][1]]),), dtype) for u in range(n)
        ]

    merged = pl.pallas_call(
        kernel,
        out_shape=[jax.ShapeDtypeStruct((DB, FB), BF)] * 3,
        in_specs=[pl.BlockSpec(memory_space=pltpu.SMEM), vm, vm, hbm, hbm, hbm],
        out_specs=[vm] * 3,
        scratch_shapes=[
            weight, weight, weight, pltpu.VMEM((RUNS, DB, 128), BF),
            pltpu.VMEM((2, 16, 16, 256), BF), pltpu.VMEM((2, 16, 16, 256), BF),
            pltpu.VMEM((RUNS, TOK, 384), BF), pltpu.VMEM((RUNS, TOK, 384), BF),
            pltpu.VMEM((RUNS, 384, TOK), BF), pltpu.VMEM((RUNS, 384, TOK), BF),
            pltpu.VMEM((256, 384), BF),
            *([pltpu.VMEM((DB, FB), F32)] * 3), pltpu.VMEM((DB, 128), F32),
            *([pltpu.VMEM((DB, FB), F32)] * 3), pltpu.VMEM((DB, 128), F32),
            sem((3,)), sem((2, 15)), sem((2, 15)), sem((2, 16)), sem((2, 16)),
            sem((n, 2)), sem((n, 2)), sem((n, 7)), sem((n, 7)), sem((n,)), sem((n,)),
            sem((n, 7)), sem((n, 7)), sem((n, 8)), sem((n, 8)),
            *each(lambda c: (TOK,), BF), *each(lambda c: (TOK,), BF), *each(lambda c: (TOK,), F32),
            *each(lambda c: (c, TOK), BF), *each(lambda c: (7, c, 16), BF), *each(lambda c: (2, c, 16), BF),
            *each(lambda c: (c, 16), F32), *each(lambda c: (c, 16), BF), *each(lambda c: (16,), BF),
            *each(lambda c: (2, TOK), BF),
        ],
        compiler_params=pltpu.CompilerParams(
            collective_id=0, has_side_effects=True, vmem_limit_bytes=60 * 1024 * 1024
        ),
        cost_estimate=pl.CostEstimate(flops=1100000000, bytes_accessed=5200000, transcendentals=300000),
    )(token_ids, table, cotangent, gate_weight, up_weight, down_weight)
    return pl.pallas_call(
        deliver,
        out_shape=[jax.ShapeDtypeStruct((DB, FB), BF)] * 3,
        in_specs=[vm] * 3,
        out_specs=[hbm] * 3,
        scratch_shapes=[sem((3,))],
    )(*merged)


def solution(mesh):
    return jax.shard_map(
        on_device,
        mesh=mesh,
        in_specs=(
            P("fsdp", "run"),
            P(None, "fsdp"),
            P(None, "fsdp", "run"),
            P(None, "run", "fsdp"),
            P(None, "run", "fsdp"),
            P(None, "run", "fsdp"),
        ),
        out_specs=(P("run", "fsdp"), P("run", "fsdp"), P("run", "fsdp")),
        check_vma=False,
    )
```

```python
import jax
import jax.numpy as jnp
from jax import lax
from jax.experimental import pallas as pl
from jax.experimental.pallas import tpu as pltpu
from jax.sharding import PartitionSpec as P

D = 4608
FF = 18432
PRIOR = 0.01
DB = 288
FB = 576
RUNS = 4
TOK = 128
NY = 8
MESH = pl.DeviceIdType.MESH
BF = jnp.bfloat16
F32 = jnp.float32
BLOCKS = ((0, 256, 0), (256, 128, 0), (384, 128, 1))
UNITS = (
    (1, 1, True, True, True, True),
    (1, 0, False, False, False, False),
    (0, 2, True, True, True, True),
    (1, 2, True, True, True, True),
    (0, 1, False, False, False, False),
    (0, 0, False, False, False, False),
)
SIGNS = (1, -1, 1, -1, 1, -1)
EARLY = (1,)
SCHEDULE = (
    (0, 1), (1, 0), (2, 1), (4, 0), (0, 2), (3, 1), (2, 2), (1, 1), (0, 3), (3, 2),
    (4, 1), (2, 3), (5, 0), (0, 4), (1, 3), (1, 4), (3, 3), (4, 3), (4, 4), (2, 4),
    (0, 5), (5, 1), (3, 4), (1, 6), (2, 5), (4, 6), (3, 5), (0, 6), (5, 3), (5, 4),
    (2, 6), (3, 6), (1, 8), (0, 7), (5, 6), (2, 7), (4, 8), (3, 7), (1, 9), (0, 8),
    (5, 8), (0, 9), (4, 9), (2, 8), (2, 9), (3, 8), (3, 9), (5, 9),
)


def gu_lanes(block):
    return 2 * block[1] + 128 * block[2]


def all_lanes(block):
    return 3 * block[1] + 256 * block[2]


def dot(a, b):
    return jnp.dot(a, b, preferred_element_type=F32)


def iota(shape, dim):
    return lax.broadcasted_iota(jnp.int32, shape, dim)


def place(rows, shift):
    return (iota((rows, 128), 1) == iota((rows, 128), 0) + shift).astype(BF)


def act_grads(gate, up, back):
    c = 0.7978845608028654
    inner = c * (gate + 0.044715 * gate * gate * gate)
    th = jnp.tanh(inner)
    half = 0.5 * (1.0 + th)
    act = gate * half
    slope = half + 0.5 * gate * (1.0 - th * th) * c * (1.0 + 3 * 0.044715 * gate * gate)
    return act * up, back * up * slope, back * act


def kernel(
    ids_hbm, table_hbm, cot_hbm, wg_hbm, wu_hbm, wd_hbm,
    og_ref, ou_ref, od_ref,
    ids_ref, table_ref, cot_ref, wg, wu, wd, wt, m1, m2, rows_s, cot_s, rows_t, cot_t, tbl,
    num_g, num_u, num_d, num_t, den_g, den_u, den_d, den_t,
    w_sem, g_send, g_recv, f_send, f_recv, x_send, x_recv, y_send, y_recv, c_send, c_recv,
    ay_send, ay_recv, ax_send, ax_recv, *bufs,
):
    n = len(UNITS)
    sx, rx, own, sy, ry, cy, ty, tb, rt, hb = (bufs[n * i:n * i + n] for i in range(10))
    run, fs = lax.axis_index("run"), lax.axis_index("fsdp")
    y, xl = run // 2, run % 2
    chip, core = fs // 2, fs % 2
    xh, z = chip // 8, chip % 8

    def y_peer(k):
        return (lax.rem(y + NY + k, NY) * 2 + xl, fs)

    x_peer = (y * 2 + 1 - xl, fs)
    sibling = (run, chip * 2 + 1 - core)
    gather_peers, gather_chips = [], []
    for dz in (4, 3, 5, 2, 6, 1, 7, 0):
        for dx in (1, 0):
            if dz or dx:
                to = lax.rem(xh + dx, 2) * 8 + lax.rem(z + dz, 8)
                gather_peers.append((run, to * 2 + core))
                gather_chips.append(lax.rem(xh + dx, 2) * 8 + lax.rem(z + 8 - dz, 8))

    barrier = pltpu.get_barrier_semaphore()
    everyone = gather_peers + [sibling, x_peer] + [y_peer(k) for k in (-2, 2, -1, 1)]
    for peer in everyone:
        pl.semaphore_signal(barrier, inc=1, device_id=peer, device_id_type=MESH)

    small_copies = []
    for i, (src, dst) in enumerate(((ids_hbm, ids_ref), (table_hbm, table_ref), (cot_hbm, cot_ref))):
        copy = pltpu.make_async_copy(src, dst, w_sem.at[3 + i])
        copy.start()
        small_copies.append(copy)
    weight_copies = []
    for i, (src, dst) in enumerate(((wg_hbm, wg), (wu_hbm, wu), (wd_hbm, wd))):
        copy = pltpu.make_async_copy(src, dst, w_sem.at[i])
        copy.start()
        weight_copies.append(copy)

    for copy in small_copies:
        copy.wait()
    table = table_ref[...].astype(F32)
    cot = jnp.concatenate([cot_ref[r].astype(F32) for r in range(RUNS)], axis=0)
    ids = jnp.zeros((16, 128), F32)
    row, lane = iota((16, 128), 0), iota((16, 128), 1)
    for r in range(RUNS):
        for t in range(4):
            ids = jnp.where((row == 4 * r + t) & (lane == 64), ids_ref[r, t].astype(F32), ids)
    tail = dot(cot[:, 256:288].astype(BF), place(32, 32))
    table_tail = dot(table[:, 256:288].astype(BF), place(32, 0))
    tail = tail + ids + jnp.concatenate([table_tail, jnp.zeros((8, 128), F32)], axis=0)
    folded = jnp.concatenate([table[:, 0:128], table[:, 128:256]], axis=0)
    m1[core, chip] = jnp.concatenate([folded, tail], axis=1).astype(BF)
    m2[core, chip] = cot[:, 0:256].astype(BF)

    pl.semaphore_wait(barrier, len(everyone))

    sends = []

    def send(src, dst, s_sem, r_sem, peer):
        copy = pltpu.make_async_remote_copy(
            src_ref=src, dst_ref=dst, send_sem=s_sem, recv_sem=r_sem, device_id=peer, device_id_type=MESH
        )
        copy.start()
        sends.append(copy)
        return copy

    def hand_over(j, buf, i, place):
        return send(buf.at[core, place], buf.at[core, place], f_send.at[j, i], f_recv.at[j, i], sibling)

    gathers = []
    for j, buf in enumerate((m1, m2)):
        gathers.append([
            send(buf.at[core, chip], buf.at[core, chip], g_send.at[j, i], g_recv.at[j, i], peer)
            for i, peer in enumerate(gather_peers)
        ])

    for copy in weight_copies:
        copy.wait()
    for r in range(RUNS):
        wt[r] = jnp.concatenate([wg[r, :, 512:576], wu[r, :, 512:576]], axis=1)

    def finish_gather(j, buf):
        handed = [hand_over(j, buf, 15, chip)]
        for i in reversed(range(15)):
            gathers[j][i].wait_recv()
            handed.append(hand_over(j, buf, i, gather_chips[i]))
        for copy in handed:
            copy.wait_recv()

    def picker(r):
        i, g = iota((TOK, 512), 0), iota((TOK, 512), 1)
        return (g == 16 * (i // 4) + 4 * r + i % 4).astype(BF)

    finish_gather(0, m1)
    m1f = m1[...].astype(F32).reshape(32, 16, 256)
    tbl[:, 0:128] = m1f[:, 0:8, 0:128].reshape(256, 128).astype(BF)
    tbl[:, 128:256] = m1f[:, 8:16, 0:128].reshape(256, 128).astype(BF)
    tbl[:, 256:384] = m1f[:, 0:8, 128:256].reshape(256, 128).astype(BF)

    def pick_rows(r):
        z_tail = dot(picker(r), m1[...].reshape(512, 256)[:, 128:256])
        j = iota((TOK, 256), 1)
        entry = ((j % 128) // 8) * 16 + (j // 128) * 8 + j % 8
        hot = (z_tail[:, 64:65].astype(jnp.int32) == entry).astype(BF)
        rows = dot(hot, tbl[...])
        rows_s[r] = rows.astype(BF)
        rows_t[r] = rows.T.astype(BF)
        cot_tail = pltpu.roll(z_tail, 96, 1)
        cot_s[r, :, 256:384] = cot_tail.astype(BF)
        cot_t[r, 256:384, :] = cot_tail.T.astype(BF)

    def pick_cot(r):
        main = dot(picker(r), m2[...].reshape(512, 256))
        cot_s[r, :, 0:256] = main.astype(BF)
        cot_t[r, 0:256, :] = main.T.astype(BF)

    def forward_gu(r, u, out):
        first, w, last = BLOCKS[UNITS[u][1]]
        rows = rows_s[r, :, 0:DB]
        out[:, 0:w] = (dot(rows, wg[r, :, first:first + w]) * D ** -0.5).astype(out.dtype)
        out[:, w:2 * w] = (dot(rows, wu[r, :, first:first + w]) * D ** -0.5).astype(out.dtype)
        if last:
            out[:, 2 * w:2 * w + 128] = (dot(rows, wt[r]) * D ** -0.5).astype(out.dtype)

    def forward_b(r, u, out):
        block = BLOCKS[UNITS[u][1]]
        first, w, last = block
        b = gu_lanes(block)
        cots = cot_s[r, :, 0:DB]
        out[:, b:b + w] = (dot(cots, wd[r, :, first:first + w]) * FF ** -0.5).astype(out.dtype)
        if last:
            left = dot(cots, wd[r, :, 512:576]) * FF ** -0.5
            out[:, b + w:b + w + 128] = jnp.concatenate([left, jnp.zeros_like(left)], axis=1).astype(out.dtype)

    exchanges, scatters, crossings, spreads, relays = {}, {}, {}, {}, {}

    def their_run(u):
        return 2 * UNITS[u][0] + 1 - xl

    def my_run(u):
        return 2 * UNITS[u][0] + xl

    def at(k):
        return pl.ds(pl.multiple_of(16 * lax.rem(y + NY + k, NY), 16), 16)

    def start_x(u, part):
        block = BLOCKS[UNITS[u][1]]
        b = gu_lanes(block)
        lanes = (pl.ds(0, b), pl.ds(b, all_lanes(block) - b))[part]
        exchanges[u, part] = send(
            sx[u].at[:, lanes], rx[u].at[:, lanes], x_send.at[u, part], x_recv.at[u, part], x_peer
        )

    def sign(u):
        return SIGNS[u]

    def scatter(u, slot, src, to):
        scatters[u, slot] = send(src, ry[u].at[slot], y_send.at[u, slot], y_recv.at[u, slot], y_peer(to))

    def scatter_first(u):
        g = sign(u)
        direct = () if UNITS[u][3] else ((3, -1, -1), (4, 1, 1))
        for slot, owner, to in ((0, -4, -2), (1, -3, -1), (2, 3, 1)) + direct:
            scatter(u, slot, sy[u].at[:, at(g * owner)], g * to)

    def reduce_x(u):
        if UNITS[u][2]:
            return
        exchanges[u, 0].wait_recv()
        exchanges[u, 1].wait_recv()
        sy[u][0] = (own[u][...] + rx[u][...].astype(F32)).astype(BF)
        scatter_first(u)

    def add_arrived(u, owner, slots):
        total = sy[u][:, at(owner), :].astype(F32)
        for slot in slots:
            scatters[u, slot].wait_recv()
            total = total + ry[u][slot].astype(F32)
        return total

    def combine_y(u):
        g = sign(u)
        step, sent = (1, 3) if UNITS[u][3] else (2, 5)
        for i, (slots, side) in enumerate((((0, 1), -1), ((2,), 1))):
            cy[u][i] = add_arrived(u, 2 * side * g, slots).astype(BF)
            scatter(u, sent + i, cy[u].at[i], g * side * step)

    def combine_again(u):
        if UNITS[u][3]:
            g = sign(u)
            for i, side in enumerate((-1, 1)):
                cy[u][2 + i] = add_arrived(u, side * g, (3 + i,)).astype(BF)
                scatter(u, 5 + i, cy[u].at[2 + i], g * side)

    def finish_y(u):
        total = add_arrived(u, 0, (5, 6) if UNITS[u][3] else (3, 4, 5, 6))
        ty[u][...] = total
        if UNITS[u][2]:
            tb[u][...] = total.astype(BF)
            crossings[u] = send(tb[u].at[1 - xl], rt[u], c_send.at[u], c_recv.at[u], x_peer)

    def relay(u, slot, owner):
        block = hb[u].at[xl, at(owner)]
        relays[u].append(send(block, block, ax_send.at[u, slot], ax_recv.at[u, slot], x_peer))

    def spread(u, slot, owner, to):
        block = hb[u].at[:, at(owner)] if UNITS[u][4] else hb[u].at[xl, at(owner)]
        spreads[u, slot] = send(block, block, ay_send.at[u, slot], ay_recv.at[u, slot], y_peer(to))

    def activate(u):
        if UNITS[u][2]:
            crossings[u].wait_recv()
            total = ty[u][xl] + rt[u][...].astype(F32)
        else:
            total = ty[u][0]
        block = BLOCKS[UNITS[u][1]]
        w, b = block[1], gu_lanes(block)
        hidden, d_gate, d_up = act_grads(total[:, 0:w], total[:, w:2 * w], total[:, b:b + w])
        parts = [d_gate, d_up, hidden]
        if block[2]:
            both, back = total[:, 2 * w:2 * w + 128], total[:, b + w:b + w + 128]
            hidden, d_gate, d_up = act_grads(both, pltpu.roll(both, 64, 1), back)
            low = iota((16, 128), 1) < 64
            parts.insert(2, jnp.where(low, d_gate, pltpu.roll(d_up, 64, 1)))
            parts.append(jnp.where(low, hidden, 0.0))
        hb[u][xl, at(0), :] = jnp.concatenate(parts, axis=1).astype(BF)
        relays[u] = []
        if UNITS[u][4]:
            relay(u, 7, 0)
        else:
            spread_first(u)
            relay(u, 7, 0)

    def spread_first(u):
        g = sign(u)
        for slot, to in ((0, 1), (1, -1)) if UNITS[u][5] else ((0, 2), (1, -2), (2, 1), (3, -1)):
            spread(u, slot, 0, g * to)

    def cross_back(u):
        if UNITS[u][4]:
            relays[u][0].wait_recv()
            spread_first(u)

    def arrived(u, slot, owner):
        spreads[u, slot].wait_recv()
        if not UNITS[u][4]:
            relay(u, slot, owner)

    def pass_far(u, first, second):
        g = sign(u)
        spreads[u, first].wait_recv()
        spread(u, 5, -2 * g, 2 * g)
        spread(u, 4, -2 * g, g)
        spreads[u, second].wait_recv()
        spread(u, 6, 2 * g, -g)
        if not UNITS[u][4]:
            relay(u, first, -2 * g)
            relay(u, second, 2 * g)

    def pass_on(u):
        g = sign(u)
        if UNITS[u][5]:
            for slot, side in ((0, 1), (1, -1)):
                spreads[u, slot].wait_recv()
                spread(u, 2 + slot, -side * g, side * g)
            if not UNITS[u][4]:
                relay(u, 0, -g)
                relay(u, 1, g)
        else:
            pass_far(u, 0, 1)
            arrived(u, 2, -g)
            arrived(u, 3, g)

    def pass_again(u):
        if UNITS[u][5]:
            pass_far(u, 2, 3)

    def pass_last(u):
        g = sign(u)
        for slot, owner in ((4, -3), (6, 3), (5, -4)):
            arrived(u, slot, g * owner)

    merged_pairs = {}

    def merge(u):
        if not UNITS[u][4]:
            for copy in relays[u]:
                copy.wait_recv()
        p, which = UNITS[u][:2]
        block = BLOCKS[which]
        first, w, last = block
        b = gu_lanes(block)
        cols = slice(first, first + w)
        jobs = [
            (rows_t, slice(0, w), wg, cols, num_g, den_g, 1.0 / D, og_ref),
            (rows_t, slice(w, 2 * w), wu, cols, num_u, den_u, 1.0 / D, ou_ref),
            (cot_t, slice(b, b + w), wd, cols, num_d, den_d, 1.0 / FF, od_ref),
        ]
        if last:
            jobs.append((rows_t, slice(2 * w, 2 * w + 128), wt, slice(0, 128), num_t, den_t, 1.0 / D, None))
            jobs.append((cot_t, slice(b + w, b + w + 64), wd, slice(512, 576), num_d, den_d, 1.0 / FF, od_ref))
        for left, lanes, weight, cols, num, den, scale, out in jobs:
            n, d = None, None
            for i in range(2):
                grad = dot(left[2 * p + i, 0:DB, :], hb[u][i, :, lanes])
                factor = grad * grad * scale + PRIOR
                term = factor * weight[2 * p + i, :, cols].astype(F32)
                n, d = (term, factor) if n is None else (n + term, d + factor)
            if which not in merged_pairs:
                num[:, cols] = n
                den[:, cols] = d
                continue
            merged = ((num[:, cols] + n) / (den[:, cols] + d)).astype(BF)
            if out is None:
                og_ref[:, 512:576] = merged[:, 0:64]
                ou_ref[:, 512:576] = merged[:, 64:128]
            else:
                out[:, cols] = merged
        merged_pairs[which] = True

    have_rows, have_cot, late = set(), set(), []

    def rows_for(key, r):
        if key not in have_rows:
            have_rows.add(key)
            pick_rows(r)

    def cot_for(key, r):
        if key not in have_cot:
            have_cot.add(key)
            pick_cot(r)

    def key_of(u, other):
        return (UNITS[u][0], other)

    def gu_send(u):
        if UNITS[u][2]:
            for i in range(2):
                rows_for(key_of(u, i), 2 * UNITS[u][0] + (xl if i else 1 - xl))
            for i, r in enumerate((their_run(u), my_run(u))):
                forward_gu(r, u, sy[u].at[(1 - xl) if i == 0 else xl])
        else:
            rows_for(key_of(u, 0), their_run(u))
            forward_gu(their_run(u), u, sx[u])
            start_x(u, 0)

    def b_send(u):
        if UNITS[u][2]:
            for i in range(2):
                cot_for(key_of(u, i), 2 * UNITS[u][0] + (xl if i else 1 - xl))
            for i, r in enumerate((their_run(u), my_run(u))):
                forward_b(r, u, sy[u].at[(1 - xl) if i == 0 else xl])
            scatter_first(u)
        else:
            cot_for(key_of(u, 0), their_run(u))
            forward_b(their_run(u), u, sx[u])
            start_x(u, 1)

    def keep(u):
        if not UNITS[u][2]:
            rows_for(key_of(u, 1), my_run(u))
            cot_for(key_of(u, 1), my_run(u))
            forward_gu(my_run(u), u, own[u])
            forward_b(my_run(u), u, own[u])

    for u in EARLY:
        gu_send(u)
    finish_gather(1, m2)
    for u in range(n):
        if u not in EARLY:
            gu_send(u)
        b_send(u)
    for u in range(n):
        keep(u)

    stages = (
        reduce_x, combine_y, combine_again, finish_y, activate, cross_back, pass_on, pass_again, pass_last, merge,
    )
    for u, j in SCHEDULE:
        stages[j](u)

    for copy in sends:
        copy.wait_send()


def deliver(a, b, c, oa, ob, oc, held, in_sems, out_sems):
    parts = [(i, j, s, d) for j in range(2) for i, (s, d) in enumerate(((a, oa), (b, ob), (c, oc)))]
    copies = []
    for i, j, s, d in parts:
        rows = pl.ds(144 * j, 144)
        copies.append((
            pltpu.make_async_copy(s.at[rows], held.at[i, rows], in_sems.at[i, j]),
            pltpu.make_async_copy(held.at[i, rows], d.at[rows], out_sems.at[i, j]),
        ))
    for inward, _ in copies:
        inward.start()
    for inward, outward in copies:
        inward.wait()
        outward.start()
    for _, outward in copies:
        outward.wait()


def on_device(table, token_ids, cotangent, gate_weight, up_weight, down_weight):
    vm = pl.BlockSpec(memory_space=pltpu.VMEM)
    hbm = pl.BlockSpec(memory_space=pl.ANY)
    weight = pltpu.VMEM((RUNS, DB, FB), BF)
    sem = pltpu.SemaphoreType.DMA
    n = len(UNITS)
    runs = [2 if unit[2] else 1 for unit in UNITS]

    def each(shape_of, dtype):
        return [
            pltpu.VMEM(shape_of(runs[u]) + (all_lanes(BLOCKS[UNITS[u][1]]),), dtype) for u in range(n)
        ]

    merged = pl.pallas_call(
        kernel,
        out_shape=[jax.ShapeDtypeStruct((DB, FB), BF)] * 3,
        in_specs=[hbm] * 6,
        out_specs=[vm] * 3,
        scratch_shapes=[
            pltpu.SMEM((RUNS, 4), jnp.int32), pltpu.VMEM((8, DB), BF), pltpu.VMEM((RUNS, 4, DB), BF),
            weight, weight, weight, pltpu.VMEM((RUNS, DB, 128), BF),
            pltpu.VMEM((2, 16, 16, 256), BF), pltpu.VMEM((2, 16, 16, 256), BF),
            pltpu.VMEM((RUNS, TOK, 384), BF), pltpu.VMEM((RUNS, TOK, 384), BF),
            pltpu.VMEM((RUNS, 384, TOK), BF), pltpu.VMEM((RUNS, 384, TOK), BF),
            pltpu.VMEM((256, 384), BF),
            *([pltpu.VMEM((DB, FB), F32)] * 3), pltpu.VMEM((DB, 128), F32),
            *([pltpu.VMEM((DB, FB), F32)] * 3), pltpu.VMEM((DB, 128), F32),
            sem((6,)), sem((2, 15)), sem((2, 15)), sem((2, 16)), sem((2, 16)),
            sem((n, 2)), sem((n, 2)), sem((n, 7)), sem((n, 7)), sem((n,)), sem((n,)),
            sem((n, 7)), sem((n, 7)), sem((n, 8)), sem((n, 8)),
            *each(lambda c: (TOK,), BF), *each(lambda c: (TOK,), BF), *each(lambda c: (TOK,), F32),
            *each(lambda c: (c, TOK), BF), *each(lambda c: (7, c, 16), BF), *each(lambda c: (4, c, 16), BF),
            *each(lambda c: (c, 16), F32), *each(lambda c: (c, 16), BF), *each(lambda c: (16,), BF),
            *each(lambda c: (2, TOK), BF),
        ],
        compiler_params=pltpu.CompilerParams(
            collective_id=0, has_side_effects=True, vmem_limit_bytes=62 * 1024 * 1024
        ),
        cost_estimate=pl.CostEstimate(flops=1100000000, bytes_accessed=5200000, transcendentals=300000),
    )(token_ids, table, cotangent, gate_weight, up_weight, down_weight)
    return pl.pallas_call(
        deliver,
        out_shape=[jax.ShapeDtypeStruct((DB, FB), BF)] * 3,
        in_specs=[hbm] * 3,
        out_specs=[hbm] * 3,
        scratch_shapes=[pltpu.VMEM((3, DB, FB), BF), sem((3, 2)), sem((3, 2))],
    )(*merged)


def solution(mesh):
    return jax.shard_map(
        on_device,
        mesh=mesh,
        in_specs=(
            P("fsdp", "run"),
            P(None, "fsdp"),
            P(None, "fsdp", "run"),
            P(None, "run", "fsdp"),
            P(None, "run", "fsdp"),
            P(None, "run", "fsdp"),
        ),
        out_specs=(P("run", "fsdp"), P("run", "fsdp"), P("run", "fsdp")),
        check_vma=False,
    )
```

```python
import jax
import jax.numpy as jnp
from jax import lax
from jax.experimental import pallas as pl
from jax.experimental.pallas import tpu as pltpu
from jax.sharding import PartitionSpec as P

D = 4608
FF = 18432
PRIOR = 0.01
DB = 288
FB = 576
RUNS = 4
TOK = 128
NY = 8
MESH = pl.DeviceIdType.MESH
BF = jnp.bfloat16
F32 = jnp.float32
BLOCKS = ((0, 256, 0), (256, 128, 0), (384, 128, 1))
UNITS = (
    (1, 1, True, True, True, True),
    (1, 0, False, False, False, False),
    (0, 2, True, True, True, True),
    (1, 2, True, True, True, True),
    (0, 1, False, False, False, False),
    (0, 0, False, False, False, False),
)
SIGNS = (1, -1, 1, -1, 1, -1)
EARLY = (1,)
SCHEDULE = (
    (0, 1), (1, 0), (2, 1), (4, 0), (0, 2), (3, 1), (1, 1), (2, 2), (4, 1), (0, 3),
    (3, 2), (5, 0), (1, 3), (2, 3), (0, 4), (1, 4), (3, 3), (4, 3), (4, 4), (2, 4),
    (0, 5), (5, 1), (3, 4), (1, 6), (2, 5), (4, 6), (3, 5), (0, 6), (5, 3), (5, 4),
    (1, 8), (2, 6), (3, 6), (0, 7), (5, 6), (2, 7), (4, 8), (3, 7), (1, 9), (0, 8),
    (5, 8), (0, 9), (4, 9), (2, 8), (2, 9), (3, 8), (3, 9), (5, 9),
)


def gu_lanes(block):
    return 2 * block[1] + 128 * block[2]


def all_lanes(block):
    return 3 * block[1] + 256 * block[2]


def dot(a, b):
    return jnp.dot(a, b, preferred_element_type=F32)


def iota(shape, dim):
    return lax.broadcasted_iota(jnp.int32, shape, dim)


def place(rows, shift):
    return (iota((rows, 128), 1) == iota((rows, 128), 0) + shift).astype(BF)


def act_grads(gate, up, back):
    c = 0.7978845608028654
    inner = c * (gate + 0.044715 * gate * gate * gate)
    th = jnp.tanh(inner)
    half = 0.5 * (1.0 + th)
    act = gate * half
    slope = half + 0.5 * gate * (1.0 - th * th) * c * (1.0 + 3 * 0.044715 * gate * gate)
    return act * up, back * up * slope, back * act


def kernel(
    ids_hbm, table_hbm, cot_hbm, wg_hbm, wu_hbm, wd_hbm,
    og_ref, ou_ref, od_ref,
    ids_ref, table_ref, cot_ref, wg, wu, wd, wt, m1, m2, rows_s, cot_s, rows_t, cot_t, tbl,
    num_g, num_u, num_d, num_t, den_g, den_u, den_d, den_t,
    w_sem, g_send, g_recv, f_send, f_recv, x_send, x_recv, y_send, y_recv, c_send, c_recv,
    ay_send, ay_recv, ax_send, ax_recv, *bufs,
):
    n = len(UNITS)
    sx, rx, own, sy, ry, cy, ty, tb, rt, hb = (bufs[n * i:n * i + n] for i in range(10))
    run, fs = lax.axis_index("run"), lax.axis_index("fsdp")
    y, xl = run // 2, run % 2
    chip, core = fs // 2, fs % 2
    xh, z = chip // 8, chip % 8

    def y_peer(k):
        return (lax.rem(y + NY + k, NY) * 2 + xl, fs)

    x_peer = (y * 2 + 1 - xl, fs)
    sibling = (run, chip * 2 + 1 - core)
    gather_peers, gather_chips = [], []
    for dz in (4, 3, 5, 2, 6, 1, 7, 0):
        for dx in (1, 0):
            if dz or dx:
                to = lax.rem(xh + dx, 2) * 8 + lax.rem(z + dz, 8)
                gather_peers.append((run, to * 2 + core))
                gather_chips.append(lax.rem(xh + dx, 2) * 8 + lax.rem(z + 8 - dz, 8))

    barrier = pltpu.get_barrier_semaphore()
    everyone = gather_peers + [sibling, x_peer] + [y_peer(k) for k in (-2, 2, -1, 1)]
    for peer in everyone:
        pl.semaphore_signal(barrier, inc=1, device_id=peer, device_id_type=MESH)

    small_copies = []
    for i, (src, dst) in enumerate(((ids_hbm, ids_ref), (table_hbm, table_ref), (cot_hbm, cot_ref))):
        copy = pltpu.make_async_copy(src, dst, w_sem.at[3 + i])
        copy.start()
        small_copies.append(copy)
    weight_copies = []
    for i, (src, dst) in enumerate(((wg_hbm, wg), (wu_hbm, wu), (wd_hbm, wd))):
        copy = pltpu.make_async_copy(src, dst, w_sem.at[i])
        copy.start()
        weight_copies.append(copy)

    for copy in small_copies:
        copy.wait()
    table = table_ref[...].astype(F32)
    cot = jnp.concatenate([cot_ref[r].astype(F32) for r in range(RUNS)], axis=0)
    ids = jnp.zeros((16, 128), F32)
    row, lane = iota((16, 128), 0), iota((16, 128), 1)
    for r in range(RUNS):
        for t in range(4):
            ids = jnp.where((row == 4 * r + t) & (lane == 64), ids_ref[r, t].astype(F32), ids)
    tail = dot(cot[:, 256:288].astype(BF), place(32, 32))
    table_tail = dot(table[:, 256:288].astype(BF), place(32, 0))
    tail = tail + ids + jnp.concatenate([table_tail, jnp.zeros((8, 128), F32)], axis=0)
    folded = jnp.concatenate([table[:, 0:128], table[:, 128:256]], axis=0)
    m1[core, chip] = jnp.concatenate([folded, tail], axis=1).astype(BF)
    m2[core, chip] = cot[:, 0:256].astype(BF)

    pl.semaphore_wait(barrier, len(everyone))

    sends = []

    def send(src, dst, s_sem, r_sem, peer):
        copy = pltpu.make_async_remote_copy(
            src_ref=src, dst_ref=dst, send_sem=s_sem, recv_sem=r_sem, device_id=peer, device_id_type=MESH
        )
        copy.start()
        sends.append(copy)
        return copy

    def hand_over(j, buf, i, place):
        return send(buf.at[core, place], buf.at[core, place], f_send.at[j, i], f_recv.at[j, i], sibling)

    gathers = []
    for j, buf in enumerate((m1, m2)):
        gathers.append([
            send(buf.at[core, chip], buf.at[core, chip], g_send.at[j, i], g_recv.at[j, i], peer)
            for i, peer in enumerate(gather_peers)
        ])

    for copy in weight_copies:
        copy.wait()
    for r in range(RUNS):
        wt[r] = jnp.concatenate([wg[r, :, 512:576], wu[r, :, 512:576]], axis=1)

    def finish_gather(j, buf):
        if j == 1:
            for copy in gathers[j]:
                copy.wait_recv()
            send(buf.at[core], buf.at[core], f_send.at[j, 0], f_recv.at[j, 0], sibling).wait_recv()
            return
        handed = [hand_over(j, buf, 15, chip)]
        for i in reversed(range(15)):
            gathers[j][i].wait_recv()
            handed.append(hand_over(j, buf, i, gather_chips[i]))
        for copy in handed:
            copy.wait_recv()

    def picker(r):
        i, g = iota((TOK, 512), 0), iota((TOK, 512), 1)
        return (g == 16 * (i // 4) + 4 * r + i % 4).astype(BF)

    finish_gather(0, m1)
    m1f = m1[...].astype(F32).reshape(32, 16, 256)
    tbl[:, 0:128] = m1f[:, 0:8, 0:128].reshape(256, 128).astype(BF)
    tbl[:, 128:256] = m1f[:, 8:16, 0:128].reshape(256, 128).astype(BF)
    tbl[:, 256:384] = m1f[:, 0:8, 128:256].reshape(256, 128).astype(BF)

    def pick_rows(r):
        z_tail = dot(picker(r), m1[...].reshape(512, 256)[:, 128:256])
        j = iota((TOK, 256), 1)
        entry = ((j % 128) // 8) * 16 + (j // 128) * 8 + j % 8
        hot = (z_tail[:, 64:65].astype(jnp.int32) == entry).astype(BF)
        rows = dot(hot, tbl[...])
        rows_s[r] = rows.astype(BF)
        rows_t[r] = rows.T.astype(BF)
        cot_tail = pltpu.roll(z_tail, 96, 1)
        cot_s[r, :, 256:384] = cot_tail.astype(BF)
        cot_t[r, 256:384, :] = cot_tail.T.astype(BF)

    def pick_cot(r):
        main = dot(picker(r), m2[...].reshape(512, 256))
        cot_s[r, :, 0:256] = main.astype(BF)
        cot_t[r, 0:256, :] = main.T.astype(BF)

    def forward_gu(r, u, out):
        first, w, last = BLOCKS[UNITS[u][1]]
        rows = rows_s[r, :, 0:DB]
        out[:, 0:w] = (dot(rows, wg[r, :, first:first + w]) * D ** -0.5).astype(out.dtype)
        out[:, w:2 * w] = (dot(rows, wu[r, :, first:first + w]) * D ** -0.5).astype(out.dtype)
        if last:
            out[:, 2 * w:2 * w + 128] = (dot(rows, wt[r]) * D ** -0.5).astype(out.dtype)

    def forward_b(r, u, out):
        block = BLOCKS[UNITS[u][1]]
        first, w, last = block
        b = gu_lanes(block)
        cots = cot_s[r, :, 0:DB]
        out[:, b:b + w] = (dot(cots, wd[r, :, first:first + w]) * FF ** -0.5).astype(out.dtype)
        if last:
            left = dot(cots, wd[r, :, 512:576]) * FF ** -0.5
            out[:, b + w:b + w + 128] = jnp.concatenate([left, jnp.zeros_like(left)], axis=1).astype(out.dtype)

    exchanges, scatters, crossings, spreads, relays = {}, {}, {}, {}, {}

    def their_run(u):
        return 2 * UNITS[u][0] + 1 - xl

    def my_run(u):
        return 2 * UNITS[u][0] + xl

    def at(k):
        return pl.ds(pl.multiple_of(16 * lax.rem(y + NY + k, NY), 16), 16)

    def start_x(u, part):
        block = BLOCKS[UNITS[u][1]]
        b = gu_lanes(block)
        lanes = (pl.ds(0, b), pl.ds(b, all_lanes(block) - b))[part]
        exchanges[u, part] = send(
            sx[u].at[:, lanes], rx[u].at[:, lanes], x_send.at[u, part], x_recv.at[u, part], x_peer
        )

    def sign(u):
        return SIGNS[u]

    def scatter(u, slot, src, to):
        scatters[u, slot] = send(src, ry[u].at[slot], y_send.at[u, slot], y_recv.at[u, slot], y_peer(to))

    def scatter_first(u):
        g = sign(u)
        direct = () if UNITS[u][3] else ((3, -1, -1), (4, 1, 1))
        for slot, owner, to in ((0, -4, -2), (1, -3, -1), (2, 3, 1)) + direct:
            scatter(u, slot, sy[u].at[:, at(g * owner)], g * to)

    def reduce_x(u):
        if UNITS[u][2]:
            return
        exchanges[u, 0].wait_recv()
        exchanges[u, 1].wait_recv()
        sy[u][0] = (own[u][...] + rx[u][...].astype(F32)).astype(BF)
        scatter_first(u)

    def add_arrived(u, owner, slots):
        total = sy[u][:, at(owner), :].astype(F32)
        for slot in slots:
            scatters[u, slot].wait_recv()
            total = total + ry[u][slot].astype(F32)
        return total

    def combine_y(u):
        g = sign(u)
        step, sent = (1, 3) if UNITS[u][3] else (2, 5)
        for i, (slots, side) in enumerate((((0, 1), -1), ((2,), 1))):
            cy[u][i] = add_arrived(u, 2 * side * g, slots).astype(BF)
            scatter(u, sent + i, cy[u].at[i], g * side * step)

    def combine_again(u):
        if UNITS[u][3]:
            g = sign(u)
            for i, side in enumerate((-1, 1)):
                cy[u][2 + i] = add_arrived(u, side * g, (3 + i,)).astype(BF)
                scatter(u, 5 + i, cy[u].at[2 + i], g * side)

    def finish_y(u):
        total = add_arrived(u, 0, (5, 6) if UNITS[u][3] else (3, 4, 5, 6))
        ty[u][...] = total
        if UNITS[u][2]:
            tb[u][...] = total.astype(BF)
            crossings[u] = send(tb[u].at[1 - xl], rt[u], c_send.at[u], c_recv.at[u], x_peer)

    def relay(u, slot, owner):
        block = hb[u].at[xl, at(owner)]
        relays[u].append(send(block, block, ax_send.at[u, slot], ax_recv.at[u, slot], x_peer))

    def spread(u, slot, owner, to):
        block = hb[u].at[:, at(owner)] if UNITS[u][4] else hb[u].at[xl, at(owner)]
        spreads[u, slot] = send(block, block, ay_send.at[u, slot], ay_recv.at[u, slot], y_peer(to))

    def activate(u):
        if UNITS[u][2]:
            crossings[u].wait_recv()
            total = ty[u][xl] + rt[u][...].astype(F32)
        else:
            total = ty[u][0]
        block = BLOCKS[UNITS[u][1]]
        w, b = block[1], gu_lanes(block)
        hidden, d_gate, d_up = act_grads(total[:, 0:w], total[:, w:2 * w], total[:, b:b + w])
        parts = [d_gate, d_up, hidden]
        if block[2]:
            both, back = total[:, 2 * w:2 * w + 128], total[:, b + w:b + w + 128]
            hidden, d_gate, d_up = act_grads(both, pltpu.roll(both, 64, 1), back)
            low = iota((16, 128), 1) < 64
            parts.insert(2, jnp.where(low, d_gate, pltpu.roll(d_up, 64, 1)))
            parts.append(jnp.where(low, hidden, 0.0))
        hb[u][xl, at(0), :] = jnp.concatenate(parts, axis=1).astype(BF)
        relays[u] = []
        if UNITS[u][4]:
            relay(u, 7, 0)
        else:
            spread_first(u)
            relay(u, 7, 0)

    def spread_first(u):
        g = sign(u)
        for slot, to in ((0, 1), (1, -1)) if UNITS[u][5] else ((0, 2), (1, -2), (2, 1), (3, -1)):
            spread(u, slot, 0, g * to)

    def cross_back(u):
        if UNITS[u][4]:
            relays[u][0].wait_recv()
            spread_first(u)

    def arrived(u, slot, owner):
        spreads[u, slot].wait_recv()
        if not UNITS[u][4]:
            relay(u, slot, owner)

    def pass_far(u, first, second):
        g = sign(u)
        spreads[u, first].wait_recv()
        spread(u, 5, -2 * g, 2 * g)
        spread(u, 4, -2 * g, g)
        spreads[u, second].wait_recv()
        spread(u, 6, 2 * g, -g)
        if not UNITS[u][4]:
            relay(u, first, -2 * g)
            relay(u, second, 2 * g)

    def pass_on(u):
        g = sign(u)
        if UNITS[u][5]:
            for slot, side in ((0, 1), (1, -1)):
                spreads[u, slot].wait_recv()
                spread(u, 2 + slot, -side * g, side * g)
            if not UNITS[u][4]:
                relay(u, 0, -g)
                relay(u, 1, g)
        else:
            pass_far(u, 0, 1)
            arrived(u, 2, -g)
            arrived(u, 3, g)

    def pass_again(u):
        if UNITS[u][5]:
            pass_far(u, 2, 3)

    def pass_last(u):
        g = sign(u)
        for slot, owner in ((4, -3), (6, 3), (5, -4)):
            arrived(u, slot, g * owner)

    merged_pairs = {}

    def merge(u):
        if not UNITS[u][4]:
            for copy in relays[u]:
                copy.wait_recv()
        p, which = UNITS[u][:2]
        block = BLOCKS[which]
        first, w, last = block
        b = gu_lanes(block)
        cols = slice(first, first + w)
        jobs = [
            (rows_t, slice(0, w), wg, cols, num_g, den_g, 1.0 / D, og_ref),
            (rows_t, slice(w, 2 * w), wu, cols, num_u, den_u, 1.0 / D, ou_ref),
            (cot_t, slice(b, b + w), wd, cols, num_d, den_d, 1.0 / FF, od_ref),
        ]
        if last:
            jobs.append((rows_t, slice(2 * w, 2 * w + 128), wt, slice(0, 128), num_t, den_t, 1.0 / D, None))
            jobs.append((cot_t, slice(b + w, b + w + 64), wd, slice(512, 576), num_d, den_d, 1.0 / FF, od_ref))
        for left, lanes, weight, cols, num, den, scale, out in jobs:
            n, d = None, None
            for i in range(2):
                grad = dot(left[2 * p + i, 0:DB, :], hb[u][i, :, lanes])
                factor = grad * grad * scale + PRIOR
                term = factor * weight[2 * p + i, :, cols].astype(F32)
                n, d = (term, factor) if n is None else (n + term, d + factor)
            if which not in merged_pairs:
                num[:, cols] = n
                den[:, cols] = d
                continue
            merged = ((num[:, cols] + n) / (den[:, cols] + d)).astype(BF)
            if out is None:
                og_ref[:, 512:576] = merged[:, 0:64]
                ou_ref[:, 512:576] = merged[:, 64:128]
            else:
                out[:, cols] = merged
        merged_pairs[which] = True

    have_rows, have_cot, late = set(), set(), []

    def rows_for(key, r):
        if key not in have_rows:
            have_rows.add(key)
            pick_rows(r)

    def cot_for(key, r):
        if key not in have_cot:
            have_cot.add(key)
            pick_cot(r)

    def key_of(u, other):
        return (UNITS[u][0], other)

    def gu_send(u):
        if UNITS[u][2]:
            for i in range(2):
                rows_for(key_of(u, i), 2 * UNITS[u][0] + (xl if i else 1 - xl))
            for i, r in enumerate((their_run(u), my_run(u))):
                forward_gu(r, u, sy[u].at[(1 - xl) if i == 0 else xl])
        else:
            rows_for(key_of(u, 0), their_run(u))
            forward_gu(their_run(u), u, sx[u])
            start_x(u, 0)

    def b_send(u):
        if UNITS[u][2]:
            for i in range(2):
                cot_for(key_of(u, i), 2 * UNITS[u][0] + (xl if i else 1 - xl))
            for i, r in enumerate((their_run(u), my_run(u))):
                forward_b(r, u, sy[u].at[(1 - xl) if i == 0 else xl])
            scatter_first(u)
        else:
            cot_for(key_of(u, 0), their_run(u))
            forward_b(their_run(u), u, sx[u])
            start_x(u, 1)

    def keep(u):
        if not UNITS[u][2]:
            rows_for(key_of(u, 1), my_run(u))
            cot_for(key_of(u, 1), my_run(u))
            forward_gu(my_run(u), u, own[u])
            forward_b(my_run(u), u, own[u])

    for u in EARLY:
        gu_send(u)
    finish_gather(1, m2)
    for u in EARLY:
        b_send(u)
    for u in range(n):
        if u not in EARLY:
            gu_send(u)
            b_send(u)
    for u in range(n):
        keep(u)

    stages = (
        reduce_x, combine_y, combine_again, finish_y, activate, cross_back, pass_on, pass_again, pass_last, merge,
    )
    issued, waited = [], 0
    for step, (u, j) in enumerate(SCHEDULE):
        issued.append(len(sends))
        if step >= 8:
            for copy in sends[waited:issued[step - 8]]:
                copy.wait_send()
            waited = issued[step - 8]
        stages[j](u)

    for copy in sends[waited:]:
        copy.wait_send()


def deliver(a, b, c, oa, ob, oc, held, in_sems, out_sems):
    parts = [(i, j, s, d) for j in range(2) for i, (s, d) in enumerate(((a, oa), (b, ob), (c, oc)))]
    copies = []
    for i, j, s, d in parts:
        rows = pl.ds(144 * j, 144)
        copies.append((
            pltpu.make_async_copy(s.at[rows], held.at[i, rows], in_sems.at[i, j]),
            pltpu.make_async_copy(held.at[i, rows], d.at[rows], out_sems.at[i, j]),
        ))
    for inward, _ in copies:
        inward.start()
    for inward, outward in copies:
        inward.wait()
        outward.start()
    for _, outward in copies:
        outward.wait()


def on_device(table, token_ids, cotangent, gate_weight, up_weight, down_weight):
    vm = pl.BlockSpec(memory_space=pltpu.VMEM)
    hbm = pl.BlockSpec(memory_space=pl.ANY)
    weight = pltpu.VMEM((RUNS, DB, FB), BF)
    sem = pltpu.SemaphoreType.DMA
    n = len(UNITS)
    runs = [2 if unit[2] else 1 for unit in UNITS]

    def each(shape_of, dtype):
        return [
            pltpu.VMEM(shape_of(runs[u]) + (all_lanes(BLOCKS[UNITS[u][1]]),), dtype) for u in range(n)
        ]

    merged = pl.pallas_call(
        kernel,
        out_shape=[jax.ShapeDtypeStruct((DB, FB), BF)] * 3,
        in_specs=[hbm] * 6,
        out_specs=[vm] * 3,
        scratch_shapes=[
            pltpu.SMEM((RUNS, 4), jnp.int32), pltpu.VMEM((8, DB), BF), pltpu.VMEM((RUNS, 4, DB), BF),
            weight, weight, weight, pltpu.VMEM((RUNS, DB, 128), BF),
            pltpu.VMEM((2, 16, 16, 256), BF), pltpu.VMEM((2, 16, 16, 256), BF),
            pltpu.VMEM((RUNS, TOK, 384), BF), pltpu.VMEM((RUNS, TOK, 384), BF),
            pltpu.VMEM((RUNS, 384, TOK), BF), pltpu.VMEM((RUNS, 384, TOK), BF),
            pltpu.VMEM((256, 384), BF),
            *([pltpu.VMEM((DB, FB), F32)] * 3), pltpu.VMEM((DB, 128), F32),
            *([pltpu.VMEM((DB, FB), F32)] * 3), pltpu.VMEM((DB, 128), F32),
            sem((6,)), sem((2, 15)), sem((2, 15)), sem((2, 16)), sem((2, 16)),
            sem((n, 2)), sem((n, 2)), sem((n, 7)), sem((n, 7)), sem((n,)), sem((n,)),
            sem((n, 7)), sem((n, 7)), sem((n, 8)), sem((n, 8)),
            *each(lambda c: (TOK,), BF), *each(lambda c: (TOK,), BF), *each(lambda c: (TOK,), F32),
            *each(lambda c: (c, TOK), BF), *each(lambda c: (7, c, 16), BF), *each(lambda c: (4, c, 16), BF),
            *each(lambda c: (c, 16), F32), *each(lambda c: (c, 16), BF), *each(lambda c: (16,), BF),
            *each(lambda c: (2, TOK), BF),
        ],
        compiler_params=pltpu.CompilerParams(
            collective_id=0, has_side_effects=True, vmem_limit_bytes=62 * 1024 * 1024
        ),
        cost_estimate=pl.CostEstimate(flops=1100000000, bytes_accessed=5200000, transcendentals=300000),
    )(token_ids, table, cotangent, gate_weight, up_weight, down_weight)
    return pl.pallas_call(
        deliver,
        out_shape=[jax.ShapeDtypeStruct((DB, FB), BF)] * 3,
        in_specs=[hbm] * 3,
        out_specs=[hbm] * 3,
        scratch_shapes=[pltpu.VMEM((3, DB, FB), BF), sem((3, 2)), sem((3, 2))],
    )(*merged)


def solution(mesh):
    return jax.shard_map(
        on_device,
        mesh=mesh,
        in_specs=(
            P("fsdp", "run"),
            P(None, "fsdp"),
            P(None, "fsdp", "run"),
            P(None, "run", "fsdp"),
            P(None, "run", "fsdp"),
            P(None, "run", "fsdp"),
        ),
        out_specs=(P("run", "fsdp"), P("run", "fsdp"), P("run", "fsdp")),
        check_vma=False,
    )
```

```python
import jax
import jax.numpy as jnp
from jax import lax
from jax.experimental import pallas as pl
from jax.experimental.pallas import tpu as pltpu
from jax.sharding import PartitionSpec as P

D = 4608
FF = 18432
PRIOR = 0.01
DB = 288
FB = 576
RUNS = 4
TOK = 128
NY = 8
MESH = pl.DeviceIdType.MESH
BF = jnp.bfloat16
F32 = jnp.float32
BLOCKS = ((0, 256, 0), (256, 128, 0), (384, 128, 1))
UNITS = (
    (1, 1, True, True, True, True),
    (1, 0, False, False, False, False),
    (0, 2, True, True, True, True),
    (1, 2, True, True, True, True),
    (0, 1, False, False, False, False),
    (0, 0, False, False, False, False),
)
SIGNS = (1, -1, 1, -1, 1, -1)
EARLY = (1,)
SCHEDULE = (
    (0, 1), (1, 0), (2, 1), (4, 0), (0, 2), (3, 1), (1, 1), (2, 2), (4, 1), (0, 3),
    (3, 2), (5, 0), (1, 3), (2, 3), (0, 4), (1, 4), (3, 3), (4, 3), (4, 4), (2, 4),
    (0, 5), (5, 1), (3, 4), (1, 6), (2, 5), (4, 6), (3, 5), (0, 6), (5, 3), (5, 4),
    (1, 8), (2, 6), (3, 6), (0, 7), (5, 6), (2, 7), (4, 8), (3, 7), (1, 9), (0, 8),
    (5, 8), (0, 9), (4, 9), (2, 8), (2, 9), (3, 8), (3, 9), (5, 9),
)


def gu_lanes(block):
    return 2 * block[1] + 128 * block[2]


def all_lanes(block):
    return 3 * block[1] + 256 * block[2]


def dot(a, b):
    return jnp.dot(a, b, preferred_element_type=F32)


def iota(shape, dim):
    return lax.broadcasted_iota(jnp.int32, shape, dim)


def place(rows, shift):
    return (iota((rows, 128), 1) == iota((rows, 128), 0) + shift).astype(BF)


def act_grads(gate, up, back):
    c = 0.7978845608028654
    inner = c * (gate + 0.044715 * gate * gate * gate)
    th = jnp.tanh(inner)
    half = 0.5 * (1.0 + th)
    act = gate * half
    slope = half + 0.5 * gate * (1.0 - th * th) * c * (1.0 + 3 * 0.044715 * gate * gate)
    return act * up, back * up * slope, back * act


def kernel(
    ids_hbm, table_hbm, cot_hbm, wg_hbm, wu_hbm, wd_hbm,
    og_ref, ou_ref, od_ref,
    ids_ref, table_ref, cot_ref, wg, wu, wd, wt, m1, m2, rows_s, cot_s, rows_t, cot_t, tbl,
    num_g, num_u, num_d, num_t, den_g, den_u, den_d, den_t,
    w_sem, g_send, g_recv, f_send, f_recv, x_send, x_recv, y_send, y_recv, c_send, c_recv,
    ay_send, ay_recv, ax_send, ax_recv, *bufs,
):
    n = len(UNITS)
    sx, rx, own, sy, ry, cy, ty, tb, rt, hb = (bufs[n * i:n * i + n] for i in range(10))
    run, fs = lax.axis_index("run"), lax.axis_index("fsdp")
    y, xl = run // 2, run % 2
    chip, core = fs // 2, fs % 2
    xh, z = chip // 8, chip % 8

    def y_peer(k):
        return (lax.rem(y + NY + k, NY) * 2 + xl, fs)

    x_peer = (y * 2 + 1 - xl, fs)
    sibling = (run, chip * 2 + 1 - core)
    gather_peers, gather_chips = [], []
    for dz in (4, 3, 5, 2, 6, 1, 7, 0):
        for dx in (1, 0):
            if dz or dx:
                to = lax.rem(xh + dx, 2) * 8 + lax.rem(z + dz, 8)
                gather_peers.append((run, to * 2 + core))
                gather_chips.append(lax.rem(xh + dx, 2) * 8 + lax.rem(z + 8 - dz, 8))

    barrier = pltpu.get_barrier_semaphore()
    everyone = gather_peers + [sibling, x_peer] + [y_peer(k) for k in (-2, 2, -1, 1)]
    for peer in everyone:
        pl.semaphore_signal(barrier, inc=1, device_id=peer, device_id_type=MESH)

    small_copies = []
    for i, (src, dst) in enumerate(((ids_hbm, ids_ref), (table_hbm, table_ref), (cot_hbm, cot_ref))):
        copy = pltpu.make_async_copy(src, dst, w_sem.at[3 + i])
        copy.start()
        small_copies.append(copy)
    weight_copies = []
    for i, (src, dst) in enumerate(((wg_hbm, wg), (wu_hbm, wu), (wd_hbm, wd))):
        copy = pltpu.make_async_copy(src, dst, w_sem.at[i])
        copy.start()
        weight_copies.append(copy)

    for copy in small_copies:
        copy.wait()
    table = table_ref[...].astype(F32)
    cot = jnp.concatenate([cot_ref[r].astype(F32) for r in range(RUNS)], axis=0)
    ids = jnp.zeros((16, 128), F32)
    row, lane = iota((16, 128), 0), iota((16, 128), 1)
    for r in range(RUNS):
        for t in range(4):
            ids = jnp.where((row == 4 * r + t) & (lane == 64), ids_ref[r, t].astype(F32), ids)
    tail = dot(cot[:, 256:288].astype(BF), place(32, 32))
    table_tail = dot(table[:, 256:288].astype(BF), place(32, 0))
    tail = tail + ids + jnp.concatenate([table_tail, jnp.zeros((8, 128), F32)], axis=0)
    folded = jnp.concatenate([table[:, 0:128], table[:, 128:256]], axis=0)
    m1[core, chip] = jnp.concatenate([folded, tail], axis=1).astype(BF)
    m2[core, chip] = cot[:, 0:256].astype(BF)

    pl.semaphore_wait(barrier, len(everyone))

    sends = []

    def send(src, dst, s_sem, r_sem, peer):
        copy = pltpu.make_async_remote_copy(
            src_ref=src, dst_ref=dst, send_sem=s_sem, recv_sem=r_sem, device_id=peer, device_id_type=MESH
        )
        copy.start()
        sends.append(copy)
        return copy

    def hand_over(j, buf, i, place):
        return send(buf.at[core, place], buf.at[core, place], f_send.at[j, i], f_recv.at[j, i], sibling)

    gathers = []
    for j, buf in enumerate((m1, m2)):
        gathers.append([
            send(buf.at[core, chip], buf.at[core, chip], g_send.at[j, i], g_recv.at[j, i], peer)
            for i, peer in enumerate(gather_peers)
        ])

    for copy in weight_copies:
        copy.wait()
    for r in range(RUNS):
        wt[r] = jnp.concatenate([wg[r, :, 512:576], wu[r, :, 512:576]], axis=1)

    def finish_gather(j, buf):
        if j == 1:
            for copy in gathers[j]:
                copy.wait_recv()
            send(buf.at[core], buf.at[core], f_send.at[j, 0], f_recv.at[j, 0], sibling).wait_recv()
            return
        handed = [hand_over(j, buf, 15, chip)]
        for i in reversed(range(15)):
            gathers[j][i].wait_recv()
            handed.append(hand_over(j, buf, i, gather_chips[i]))
        for copy in handed:
            copy.wait_recv()

    def picker(r):
        i, g = iota((TOK, 512), 0), iota((TOK, 512), 1)
        return (g == 16 * (i // 4) + 4 * r + i % 4).astype(BF)

    finish_gather(0, m1)
    m1f = m1[...].astype(F32).reshape(32, 16, 256)
    tbl[:, 0:128] = m1f[:, 0:8, 0:128].reshape(256, 128).astype(BF)
    tbl[:, 128:256] = m1f[:, 8:16, 0:128].reshape(256, 128).astype(BF)
    tbl[:, 256:384] = m1f[:, 0:8, 128:256].reshape(256, 128).astype(BF)

    def pick_rows(r):
        z_tail = dot(picker(r), m1[...].reshape(512, 256)[:, 128:256])
        j = iota((TOK, 256), 1)
        entry = ((j % 128) // 8) * 16 + (j // 128) * 8 + j % 8
        hot = (z_tail[:, 64:65].astype(jnp.int32) == entry).astype(BF)
        rows = dot(hot, tbl[...])
        rows_s[r] = rows.astype(BF)
        cot_tail = pltpu.roll(z_tail, 96, 1)
        cot_s[r, :, 256:384] = cot_tail.astype(BF)

    def pick_cot(r):
        main = dot(picker(r), m2[...].reshape(512, 256))
        cot_s[r, :, 0:256] = main.astype(BF)

    def forward_gu(r, u, out):
        first, w, last = BLOCKS[UNITS[u][1]]
        rows = rows_s[r, :, 0:DB]
        out[:, 0:w] = (dot(rows, wg[r, :, first:first + w]) * D ** -0.5).astype(out.dtype)
        out[:, w:2 * w] = (dot(rows, wu[r, :, first:first + w]) * D ** -0.5).astype(out.dtype)
        if last:
            out[:, 2 * w:2 * w + 128] = (dot(rows, wt[r]) * D ** -0.5).astype(out.dtype)

    def forward_b(r, u, out):
        block = BLOCKS[UNITS[u][1]]
        first, w, last = block
        b = gu_lanes(block)
        cots = cot_s[r, :, 0:DB]
        out[:, b:b + w] = (dot(cots, wd[r, :, first:first + w]) * FF ** -0.5).astype(out.dtype)
        if last:
            left = dot(cots, wd[r, :, 512:576]) * FF ** -0.5
            out[:, b + w:b + w + 128] = jnp.concatenate([left, jnp.zeros_like(left)], axis=1).astype(out.dtype)

    exchanges, scatters, crossings, spreads, relays = {}, {}, {}, {}, {}

    def their_run(u):
        return 2 * UNITS[u][0] + 1 - xl

    def my_run(u):
        return 2 * UNITS[u][0] + xl

    def at(k):
        return pl.ds(pl.multiple_of(16 * lax.rem(y + NY + k, NY), 16), 16)

    def start_x(u, part):
        block = BLOCKS[UNITS[u][1]]
        b = gu_lanes(block)
        lanes = (pl.ds(0, b), pl.ds(b, all_lanes(block) - b))[part]
        exchanges[u, part] = send(
            sx[u].at[:, lanes], rx[u].at[:, lanes], x_send.at[u, part], x_recv.at[u, part], x_peer
        )

    def sign(u):
        return SIGNS[u]

    def scatter(u, slot, src, to):
        scatters[u, slot] = send(src, ry[u].at[slot], y_send.at[u, slot], y_recv.at[u, slot], y_peer(to))

    def scatter_first(u):
        g = sign(u)
        direct = () if UNITS[u][3] else ((3, -1, -1), (4, 1, 1))
        for slot, owner, to in ((0, -4, -2), (1, -3, -1), (2, 3, 1)) + direct:
            scatter(u, slot, sy[u].at[:, at(g * owner)], g * to)

    def reduce_x(u):
        if UNITS[u][2]:
            return
        exchanges[u, 0].wait_recv()
        exchanges[u, 1].wait_recv()
        sy[u][0] = (own[u][...] + rx[u][...].astype(F32)).astype(BF)
        scatter_first(u)

    def add_arrived(u, owner, slots):
        total = sy[u][:, at(owner), :].astype(F32)
        for slot in slots:
            scatters[u, slot].wait_recv()
            total = total + ry[u][slot].astype(F32)
        return total

    def combine_y(u):
        g = sign(u)
        step, sent = (1, 3) if UNITS[u][3] else (2, 5)
        for i, (slots, side) in enumerate((((0, 1), -1), ((2,), 1))):
            cy[u][i] = add_arrived(u, 2 * side * g, slots).astype(BF)
            scatter(u, sent + i, cy[u].at[i], g * side * step)

    def combine_again(u):
        if UNITS[u][3]:
            g = sign(u)
            for i, side in enumerate((-1, 1)):
                cy[u][2 + i] = add_arrived(u, side * g, (3 + i,)).astype(BF)
                scatter(u, 5 + i, cy[u].at[2 + i], g * side)

    def finish_y(u):
        total = add_arrived(u, 0, (5, 6) if UNITS[u][3] else (3, 4, 5, 6))
        ty[u][...] = total
        if UNITS[u][2]:
            tb[u][...] = total.astype(BF)
            crossings[u] = send(tb[u].at[1 - xl], rt[u], c_send.at[u], c_recv.at[u], x_peer)

    def relay(u, slot, owner):
        block = hb[u].at[xl, at(owner)]
        relays[u].append(send(block, block, ax_send.at[u, slot], ax_recv.at[u, slot], x_peer))

    def spread(u, slot, owner, to):
        block = hb[u].at[:, at(owner)] if UNITS[u][4] else hb[u].at[xl, at(owner)]
        spreads[u, slot] = send(block, block, ay_send.at[u, slot], ay_recv.at[u, slot], y_peer(to))

    def activate(u):
        if UNITS[u][2]:
            crossings[u].wait_recv()
            total = ty[u][xl] + rt[u][...].astype(F32)
        else:
            total = ty[u][0]
        block = BLOCKS[UNITS[u][1]]
        w, b = block[1], gu_lanes(block)
        hidden, d_gate, d_up = act_grads(total[:, 0:w], total[:, w:2 * w], total[:, b:b + w])
        parts = [d_gate, d_up, hidden]
        if block[2]:
            both, back = total[:, 2 * w:2 * w + 128], total[:, b + w:b + w + 128]
            hidden, d_gate, d_up = act_grads(both, pltpu.roll(both, 64, 1), back)
            low = iota((16, 128), 1) < 64
            parts.insert(2, jnp.where(low, d_gate, pltpu.roll(d_up, 64, 1)))
            parts.append(jnp.where(low, hidden, 0.0))
        hb[u][xl, at(0), :] = jnp.concatenate(parts, axis=1).astype(BF)
        relays[u] = []
        if UNITS[u][4]:
            relay(u, 7, 0)
        else:
            spread_first(u)
            relay(u, 7, 0)

    def spread_first(u):
        g = sign(u)
        for slot, to in ((0, 1), (1, -1)) if UNITS[u][5] else ((0, 2), (1, -2), (2, 1), (3, -1)):
            spread(u, slot, 0, g * to)

    def cross_back(u):
        if UNITS[u][4]:
            relays[u][0].wait_recv()
            spread_first(u)

    def arrived(u, slot, owner):
        spreads[u, slot].wait_recv()
        if not UNITS[u][4]:
            relay(u, slot, owner)

    def pass_far(u, first, second):
        g = sign(u)
        spreads[u, first].wait_recv()
        spread(u, 5, -2 * g, 2 * g)
        spread(u, 4, -2 * g, g)
        spreads[u, second].wait_recv()
        spread(u, 6, 2 * g, -g)
        if not UNITS[u][4]:
            relay(u, first, -2 * g)
            relay(u, second, 2 * g)

    def pass_on(u):
        g = sign(u)
        if UNITS[u][5]:
            for slot, side in ((0, 1), (1, -1)):
                spreads[u, slot].wait_recv()
                spread(u, 2 + slot, -side * g, side * g)
            if not UNITS[u][4]:
                relay(u, 0, -g)
                relay(u, 1, g)
        else:
            pass_far(u, 0, 1)
            arrived(u, 2, -g)
            arrived(u, 3, g)

    def pass_again(u):
        if UNITS[u][5]:
            pass_far(u, 2, 3)

    def pass_last(u):
        g = sign(u)
        for slot, owner in ((4, -3), (6, 3), (5, -4)):
            arrived(u, slot, g * owner)

    merged_pairs = {}

    def merge(u):
        if not UNITS[u][4]:
            for copy in relays[u]:
                copy.wait_recv()
        p, which = UNITS[u][:2]
        block = BLOCKS[which]
        first, w, last = block
        b = gu_lanes(block)
        cols = slice(first, first + w)
        jobs = [
            (rows_t, slice(0, w), wg, cols, num_g, den_g, 1.0 / D, og_ref),
            (rows_t, slice(w, 2 * w), wu, cols, num_u, den_u, 1.0 / D, ou_ref),
            (cot_t, slice(b, b + w), wd, cols, num_d, den_d, 1.0 / FF, od_ref),
        ]
        if last:
            jobs.append((rows_t, slice(2 * w, 2 * w + 128), wt, slice(0, 128), num_t, den_t, 1.0 / D, None))
            jobs.append((cot_t, slice(b + w, b + w + 64), wd, slice(512, 576), num_d, den_d, 1.0 / FF, od_ref))
        for left, lanes, weight, cols, num, den, scale, out in jobs:
            n, d = None, None
            for i in range(2):
                grad = dot(left[2 * p + i, 0:DB, :], hb[u][i, :, lanes])
                factor = grad * grad * scale + PRIOR
                term = factor * weight[2 * p + i, :, cols].astype(F32)
                n, d = (term, factor) if n is None else (n + term, d + factor)
            if which not in merged_pairs:
                num[:, cols] = n
                den[:, cols] = d
                continue
            merged = ((num[:, cols] + n) / (den[:, cols] + d)).astype(BF)
            if out is None:
                og_ref[:, 512:576] = merged[:, 0:64]
                ou_ref[:, 512:576] = merged[:, 64:128]
            else:
                out[:, cols] = merged
        merged_pairs[which] = True

    have_rows, have_cot, late = set(), set(), []

    def rows_for(key, r):
        if key not in have_rows:
            have_rows.add(key)
            pick_rows(r)

    def cot_for(key, r):
        if key not in have_cot:
            have_cot.add(key)
            pick_cot(r)

    def key_of(u, other):
        return (UNITS[u][0], other)

    def gu_send(u):
        if UNITS[u][2]:
            for i in range(2):
                rows_for(key_of(u, i), 2 * UNITS[u][0] + (xl if i else 1 - xl))
            for i, r in enumerate((their_run(u), my_run(u))):
                forward_gu(r, u, sy[u].at[(1 - xl) if i == 0 else xl])
        else:
            rows_for(key_of(u, 0), their_run(u))
            forward_gu(their_run(u), u, sx[u])
            start_x(u, 0)

    def b_send(u):
        if UNITS[u][2]:
            for i in range(2):
                cot_for(key_of(u, i), 2 * UNITS[u][0] + (xl if i else 1 - xl))
            for i, r in enumerate((their_run(u), my_run(u))):
                forward_b(r, u, sy[u].at[(1 - xl) if i == 0 else xl])
            scatter_first(u)
        else:
            cot_for(key_of(u, 0), their_run(u))
            forward_b(their_run(u), u, sx[u])
            start_x(u, 1)

    def keep(u):
        if not UNITS[u][2]:
            rows_for(key_of(u, 1), my_run(u))
            cot_for(key_of(u, 1), my_run(u))
            forward_gu(my_run(u), u, own[u])
            forward_b(my_run(u), u, own[u])

    for u in EARLY:
        gu_send(u)
    finish_gather(1, m2)
    for u in EARLY:
        b_send(u)
    for u in range(n):
        if u not in EARLY:
            gu_send(u)
            b_send(u)
    for u in range(n):
        keep(u)
    for r in range(RUNS):
        rows_t[r] = rows_s[r].astype(F32).T.astype(BF)
        cot_t[r] = cot_s[r].astype(F32).T.astype(BF)

    stages = (
        reduce_x, combine_y, combine_again, finish_y, activate, cross_back, pass_on, pass_again, pass_last, merge,
    )
    issued, waited = [], 0
    for step, (u, j) in enumerate(SCHEDULE):
        issued.append(len(sends))
        if step >= 8:
            for copy in sends[waited:issued[step - 8]]:
                copy.wait_send()
            waited = issued[step - 8]
        stages[j](u)

    for copy in sends[waited:]:
        copy.wait_send()


def deliver(a, b, c, oa, ob, oc, held, in_sems, out_sems):
    parts = [(i, j, s, d) for j in range(2) for i, (s, d) in enumerate(((a, oa), (b, ob), (c, oc)))]
    copies = []
    for i, j, s, d in parts:
        rows = pl.ds(144 * j, 144)
        copies.append((
            pltpu.make_async_copy(s.at[rows], held.at[i, rows], in_sems.at[i, j]),
            pltpu.make_async_copy(held.at[i, rows], d.at[rows], out_sems.at[i, j]),
        ))
    for inward, _ in copies:
        inward.start()
    for inward, outward in copies:
        inward.wait()
        outward.start()
    for _, outward in copies:
        outward.wait()


def on_device(table, token_ids, cotangent, gate_weight, up_weight, down_weight):
    vm = pl.BlockSpec(memory_space=pltpu.VMEM)
    hbm = pl.BlockSpec(memory_space=pl.ANY)
    weight = pltpu.VMEM((RUNS, DB, FB), BF)
    sem = pltpu.SemaphoreType.DMA
    n = len(UNITS)
    runs = [2 if unit[2] else 1 for unit in UNITS]

    def each(shape_of, dtype):
        return [
            pltpu.VMEM(shape_of(runs[u]) + (all_lanes(BLOCKS[UNITS[u][1]]),), dtype) for u in range(n)
        ]

    merged = pl.pallas_call(
        kernel,
        out_shape=[jax.ShapeDtypeStruct((DB, FB), BF)] * 3,
        in_specs=[hbm] * 6,
        out_specs=[vm] * 3,
        scratch_shapes=[
            pltpu.SMEM((RUNS, 4), jnp.int32), pltpu.VMEM((8, DB), BF), pltpu.VMEM((RUNS, 4, DB), BF),
            weight, weight, weight, pltpu.VMEM((RUNS, DB, 128), BF),
            pltpu.VMEM((2, 16, 16, 256), BF), pltpu.VMEM((2, 16, 16, 256), BF),
            pltpu.VMEM((RUNS, TOK, 384), BF), pltpu.VMEM((RUNS, TOK, 384), BF),
            pltpu.VMEM((RUNS, 384, TOK), BF), pltpu.VMEM((RUNS, 384, TOK), BF),
            pltpu.VMEM((256, 384), BF),
            *([pltpu.VMEM((DB, FB), F32)] * 3), pltpu.VMEM((DB, 128), F32),
            *([pltpu.VMEM((DB, FB), F32)] * 3), pltpu.VMEM((DB, 128), F32),
            sem((6,)), sem((2, 15)), sem((2, 15)), sem((2, 16)), sem((2, 16)),
            sem((n, 2)), sem((n, 2)), sem((n, 7)), sem((n, 7)), sem((n,)), sem((n,)),
            sem((n, 7)), sem((n, 7)), sem((n, 8)), sem((n, 8)),
            *each(lambda c: (TOK,), BF), *each(lambda c: (TOK,), BF), *each(lambda c: (TOK,), F32),
            *each(lambda c: (c, TOK), BF), *each(lambda c: (7, c, 16), BF), *each(lambda c: (4, c, 16), BF),
            *each(lambda c: (c, 16), F32), *each(lambda c: (c, 16), BF), *each(lambda c: (16,), BF),
            *each(lambda c: (2, TOK), BF),
        ],
        compiler_params=pltpu.CompilerParams(
            collective_id=0, has_side_effects=True, vmem_limit_bytes=62 * 1024 * 1024
        ),
        cost_estimate=pl.CostEstimate(flops=1100000000, bytes_accessed=5200000, transcendentals=300000),
    )(token_ids, table, cotangent, gate_weight, up_weight, down_weight)
    return pl.pallas_call(
        deliver,
        out_shape=[jax.ShapeDtypeStruct((DB, FB), BF)] * 3,
        in_specs=[hbm] * 3,
        out_specs=[hbm] * 3,
        scratch_shapes=[pltpu.VMEM((3, DB, FB), BF), sem((3, 2)), sem((3, 2))],
    )(*merged)


def solution(mesh):
    return jax.shard_map(
        on_device,
        mesh=mesh,
        in_specs=(
            P("fsdp", "run"),
            P(None, "fsdp"),
            P(None, "fsdp", "run"),
            P(None, "run", "fsdp"),
            P(None, "run", "fsdp"),
            P(None, "run", "fsdp"),
        ),
        out_specs=(P("run", "fsdp"), P("run", "fsdp"), P("run", "fsdp")),
        check_vma=False,
    )
```
